128 devices in a mesh: dp: 16 (over z_hi, x, core), feat: 8 (over z_lo, y).
Axes of the slice: x: 4, y: 4, z: 4 (z_hi: 2, z_lo: 2; z = z_hi * 2 + z_lo), core: 2. Of those that a mesh axis runs over, the one named last changes fastest.
Arguments:
- view_features: bfloat16 [2, 2048, 8192], P(None, 'dp', 'feat'), may hold values from 0 to 55, as said below
- weight: float32 [8192, 8192], P('dp', 'feat'), may hold values from -64 to 64
- velocity: float32 [8192, 8192], P('dp', 'feat'), may hold values from -6 to 6
Outputs:
- new_weight: float32 [8192, 8192], P('dp', 'feat')
- new_velocity: float32 [8192, 8192], P('dp', 'feat')
The draws below stay inside these ranges and needn't reach their ends.
Inputs may be any that keep to these rules, and one draw needn't show every extreme that they name: `view_features`: nonnegative features.
All inputs are finite; a program needn't handle non-finite values.
Results may differ from the reference program's by a relative error of at most 0.039.
Values may be sent and summed in bfloat16 or wider, within the bound.
A program may use at most 128 MiB of HBM per device.

```python
import math
import jax
import jax.numpy as jnp
from jax import lax

D = 8192
IMAGES = 2048
N_DP = 16
N_FEAT = 8


def draw_view_features(key, part):
    key_shared, key_own, key_column = jax.random.split(key, 3)
    position = jnp.arange(IMAGES, dtype=jnp.float32) / max(IMAGES - 1, 1)
    column = jnp.exp(jax.random.uniform(key_column, (1, 1, D), jnp.float32, math.log(0.5), math.log(2.0)))
    shared = jax.random.truncated_normal(key_shared, -4.0, 4.0, (1, IMAGES, D), jnp.float32)
    own = jax.random.truncated_normal(key_own, -4.0, 4.0, (2, IMAGES, D), jnp.float32)
    row_scale = jnp.exp(math.log(3.0) * position)[None, :, None]
    mixed = jnp.maximum(0.95 * shared + 0.3 * own + 0.6, 0.0) * row_scale * column
    return mixed.astype(jnp.bfloat16)


def draw_weight(key, part):
    key_base, key_common = jax.random.split(key, 2)
    span = max(D - 1, 1)
    row_pos = jnp.arange(D, dtype=jnp.float32)[:, None] / span
    col_pos = jnp.arange(D, dtype=jnp.float32)[None, :] / span
    base = jax.random.truncated_normal(key_base, -4.0, 4.0, (D, D), jnp.float32)
    common = jax.random.truncated_normal(key_common, -4.0, 4.0, (D, 1), jnp.float32)
    factor = math.log(3.0)
    return (0.7 * base + 0.7 * common) * jnp.exp(0.5 * factor * (row_pos + col_pos))


def steps_of(key, extent, cuts, low, high):
    level = 1.0
    for dim, parts in cuts:
        draws = jax.random.uniform(jax.random.fold_in(jax.random.fold_in(key, 6), dim), (parts,), jnp.float32, low / len(cuts), high / len(cuts))
        level = level * jnp.repeat(jnp.exp(draws), extent[dim] // parts).reshape((-1,) + (1,) * (len(extent) - 1 - dim))
    return level


def gaussian(own_key, shape, scale, reach, cuts=(), kind=jnp.bfloat16):
    entries = jax.random.normal(own_key, shape, jnp.float32) * scale
    if len(cuts) > 0:
        entries = steps_of(own_key, shape, cuts, -0.22, 0.18) * entries
    return jnp.clip(entries, min=-reach, max=reach).astype(kind)


def setup_inputs(seed: int = 0) -> dict:
    streams_of = jax.random.split(jax.random.key(seed), 4)
    return {
        "view_features": draw_view_features(jax.random.fold_in(streams_of[3], 71), 0),
        "weight": draw_weight(jax.random.fold_in(streams_of[3], 71), 0),
        "velocity": gaussian(streams_of[2], (D, D), 1.0, 6.0, ((0, 16), (1, 8)), jnp.float32),
    }


EPSILON = 1e-05
NORM_EPSILON = 1e-06
REDUNDANCY = 0.0051
MOMENTUM = 0.9
LEARN_RATE = 0.2

def round_half(value):
    return lax.optimization_barrier(value.astype(jnp.bfloat16)).astype(jnp.float32)

def reference(view_features, weight, velocity):
    block_dp = D // N_DP
    block_feat = D // N_FEAT
    highest = lax.Precision.HIGHEST
    flat_views = view_features.reshape(2 * IMAGES, D).astype(jnp.float32)
    weight_half = round_half(weight)

    def forward_block(index_block, running):
        start_at = (index_block * block_dp).astype(jnp.int32)
        part_views = lax.dynamic_slice_in_dim(flat_views, start_at, block_dp, 1)
        part_weight = lax.dynamic_slice_in_dim(weight_half, start_at, block_dp, 0)
        return running + round_half(jnp.dot(part_views, part_weight, precision=highest))
    outputs = lax.fori_loop(0, N_DP, forward_block, jnp.zeros((2 * IMAGES, D), jnp.float32))
    outputs = outputs.reshape(2, IMAGES, D)
    average = lax.optimization_barrier(jnp.mean(outputs, axis=1, keepdims=True))
    centered = outputs - average
    variance = lax.optimization_barrier(jnp.mean(centered * centered, axis=1, keepdims=True))
    inverse = lax.rsqrt(variance + EPSILON)
    normed = centered * inverse
    normed_half = round_half(normed)
    first_view = normed_half[0]
    second_view = normed_half[1]
    correlation = jnp.dot(first_view.T, second_view, precision=highest) / IMAGES
    diagonal = jnp.eye(D, dtype=bool)
    scaled = round_half(jnp.where(diagonal, -2.0 * (1.0 - correlation), 2.0 * REDUNDANCY * correlation) / IMAGES)

    def first_block(index_block, running):
        start_at = (index_block * block_feat).astype(jnp.int32)
        part_second = lax.dynamic_slice_in_dim(second_view, start_at, block_feat, 1)
        part_scaled = lax.dynamic_slice_in_dim(scaled, start_at, block_feat, 1)
        return running + round_half(jnp.dot(part_second, part_scaled.T, precision=highest))

    def second_block(index_block, running):
        start_at = (index_block * block_dp).astype(jnp.int32)
        part_first = lax.dynamic_slice_in_dim(first_view, start_at, block_dp, 1)
        part_scaled = lax.dynamic_slice_in_dim(scaled, start_at, block_dp, 0)
        return running + round_half(jnp.dot(part_first, part_scaled, precision=highest))
    first_grad = lax.fori_loop(0, N_FEAT, first_block, jnp.zeros((IMAGES, D), jnp.float32))
    second_grad = lax.fori_loop(0, N_DP, second_block, jnp.zeros((IMAGES, D), jnp.float32))
    grads = jnp.stack([first_grad, second_grad])
    grad_mean = lax.optimization_barrier(jnp.mean(grads, axis=1, keepdims=True))
    grad_cross = lax.optimization_barrier(jnp.mean(grads * normed, axis=1, keepdims=True))
    out_grad = round_half(inverse * (grads - grad_mean - normed * grad_cross))
    weight_grad = jnp.dot(flat_views.T, out_grad.reshape(2 * IMAGES, D), precision=highest)
    weight_norm = jnp.sqrt(jnp.sum(weight * weight))
    grad_norm = jnp.sqrt(jnp.sum(weight_grad * weight_grad))
    trust = weight_norm / (grad_norm + NORM_EPSILON)
    new_velocity = MOMENTUM * velocity + trust * weight_grad
    new_weight = weight - LEARN_RATE * new_velocity
    return (new_weight, new_velocity)
```

```python
import functools

import jax
import jax.numpy as jnp
from jax import lax
from jax.experimental import pallas as pl
from jax.experimental.pallas import tpu as pltpu
from jax.sharding import PartitionSpec as P

EPSILON = 1e-05
NORM_EPSILON = 1e-06
REDUNDANCY = 0.0051
MOMENTUM = 0.9
LEARN_RATE = 0.2
MESH = pl.DeviceIdType.MESH
BF = jnp.bfloat16
F32 = jnp.float32
NCH = 4


class Place:
    def __init__(self):
        d, f = lax.axis_index("dp"), lax.axis_index("feat")
        self.d, self.f, self.p = d, f, d // 2
        self.zh, self.x, self.c = d // 8, (d // 2) % 4, d % 2
        self.zl, self.y = f // 4, f % 4

    def at(self, zh=None, x=None, c=None, zl=None, y=None):
        zh = self.zh if zh is None else zh
        x = self.x if x is None else x
        c = self.c if c is None else c
        zl = self.zl if zl is None else zl
        y = self.y if y is None else y
        return ((zh * 4 + x) * 2 + c, zl * 4 + y)


def signal(target):
    pl.semaphore_signal(
        pltpu.get_barrier_semaphore(), inc=1, device_id=target, device_id_type=MESH
    )


def remote(src, dst, send, recv, target):
    return pltpu.make_async_remote_copy(
        src_ref=src, dst_ref=dst, send_sem=send, recv_sem=recv, device_id=target, device_id_type=MESH
    )


class Gather:
    def __init__(self, q, r, device, piece, send, recv):
        up, down, far, other = (r + 1) % 4, (r + 3) % 4, (r + 2) % 4, 1 - q
        self.blocks = [
            other * 4 + r, q * 4 + down, q * 4 + up, q * 4 + far,
            other * 4 + down, other * 4 + up, other * 4 + far,
        ]
        mine = q * 4 + r

        def make(block, k, slot, target):
            ref = piece(block, k)
            return remote(ref, ref, send.at[slot, k], recv.at[slot, k], target)

        to_up, to_down, to_pair = device(q, up), device(q, down), device(other, r)
        self.copies = []
        for k in range(NCH):
            self.copies.append([
                make(mine, k, 0, to_pair),
                make(mine, k, 1, to_up),
                make(mine, k, 2, to_down),
                make(self.blocks[1], k, 3, to_up) if k % 2 == 0 else make(self.blocks[2], k, 3, to_down),
                make(self.blocks[0], k, 4, to_up),
                make(self.blocks[0], k, 5, to_down),
                make(self.blocks[3], k, 6, to_pair),
            ])

    def own(self, k):
        for slot in (0, 1, 2):
            self.copies[k][slot].start()

    def near(self, k):
        c = self.copies[k]
        c[0].wait_recv()
        c[4].start()
        c[5].start()
        c[1].wait_recv()
        c[2].wait_recv()
        c[3].start()

    def far(self, k):
        c = self.copies[k]
        c[3].wait_recv()
        c[6].start()

    def rest(self, k, slot):
        self.copies[k][slot].wait_recv()

    def close(self):
        for c in self.copies:
            for copy in c:
                copy.wait_send()


def forward_kernel(
    x_ref, w_ref, xg, normed_ref, half_ref, inv_ref,
    wf, ys, yr, zs, zr, yacc,
    perm_s, perm_r, w_s, w_r, ag_s, ag_r, rs_s, rs_r, z_s, z_r,
):
    me = Place()
    p, f, c, x, y, zh, zl = me.p, me.f, me.c, me.x, me.y, me.zh, me.zl
    same = f == p
    piece = 256 // NCH
    half = NCH // 2
    for v in range(2):
        @pl.when(jnp.logical_not(same & (c == v)))
        def _():
            signal((f * 2 + v, p))
    partners = [
        me.at(c=1 - c), me.at(y=(y + 1) % 4), me.at(y=(y + 3) % 4), me.at(zl=1 - zl),
        me.at(x=(x + 1) % 4), me.at(x=(x + 2) % 4), me.at(x=(x + 3) % 4), me.at(zh=1 - zh),
    ]
    for t in partners:
        signal(t)
    own_rows = pl.ds(pl.multiple_of(c * 512, 512), 512)
    wf[own_rows, :] = w_ref[...].astype(BF)
    pl.semaphore_wait(pltpu.get_barrier_semaphore(), len(partners) + jnp.where(same, 1, 2))

    def perm(v, h):
        src = x_ref.at[v, pl.ds(h * piece, piece)]
        dst = xg.at[p, pl.ds(pl.multiple_of((c * half + h) * piece, piece), piece)]
        return remote(src, dst, perm_s.at[v, h], perm_r.at[c * half + h], (f * 2 + v, p))

    for h in range(half):
        for v in range(2):
            here = same & (c == v)

            @pl.when(here)
            def _():
                pltpu.make_async_copy(
                    x_ref.at[v, pl.ds(h * piece, piece)],
                    xg.at[p, pl.ds(pl.multiple_of((c * half + h) * piece, piece), piece)],
                    perm_r.at[c * half + h],
                ).start()

            @pl.when(jnp.logical_not(here))
            def _():
                perm(v, h).start()

    wcopy = remote(wf.at[own_rows], wf.at[own_rows], w_s, w_r, me.at(c=1 - c))
    wcopy.start()

    ag = Gather(
        zl, y, lambda q, r: me.at(zl=q, y=r),
        lambda b, k: xg.at[b, pl.ds(k * piece, piece)], ag_s, ag_r,
    )
    for k in (0, 2, 1, 3):
        ref = xg.at[f, pl.ds(k * piece, piece)]
        pltpu.make_async_copy(ref, ref, perm_r.at[k]).wait()
        ag.own(k)
    wcopy.wait_recv()

    order = [f] + ag.blocks
    sends = []

    def product(o):
        b = order[o]

        @pl.loop(0, 4)
        def _(j):
            cols = pl.ds(pl.multiple_of(j * 256, 256), 256)
            part = jnp.dot(xg[b], wf[:, cols], preferred_element_type=F32).astype(BF)
            rows = pl.ds(pl.multiple_of(b * 256, 256), 256)
            ys[2 * (j % 2), j // 2, rows, :] = part[:, :128]
            ys[2 * (j % 2) + 1, j // 2, rows, :] = part[:, 128:]

        rows = pl.ds(pl.multiple_of(b * 256, 256), 256)
        for dx in (2, 1, 3):
            xt = (x + dx) % 4
            copy = remote(
                ys.at[xt, :, rows], yr.at[dx - 1, :, rows], rs_s.at[dx - 1, o], rs_r.at[dx - 1, o], me.at(x=xt)
            )
            copy.start()
            sends.append(copy)

    product(0)
    for k in (0, 2, 1, 3):
        ag.near(k)
    product(1)
    product(2)
    product(3)
    for k in range(NCH):
        ag.far(k)
    product(4)
    for k in range(NCH):
        ag.rest(k, 4)
    product(5)
    for k in range(NCH):
        ag.rest(k, 5)
    product(6)
    for k in range(NCH):
        ag.rest(k, 6)
    product(7)
    zcopies = []
    for o in range(8):
        rows = pl.ds(pl.multiple_of(order[o] * 256, 256), 256)
        for copy in sends[3 * o:3 * o + 3]:
            copy.wait_recv()

        def total(side):
            s = ys[x, side, rows, :].astype(F32)
            for i in range(3):
                s = s + yr[i, side, rows, :].astype(F32)
            return s

        zs[rows, :] = total(1 - zh).astype(BF)
        copy = remote(zs.at[rows], zr.at[rows], z_s.at[o], z_r.at[o], me.at(zh=1 - zh))
        copy.start()
        zcopies.append(copy)
        yacc[rows, :] = total(zh)
    for copy in zcopies:
        copy.wait_recv()
    outputs = yacc[...] + zr[...].astype(F32)
    average = jnp.sum(outputs, 0, keepdims=True) / 2048
    centered = outputs - average
    variance = jnp.sum(centered * centered, 0, keepdims=True) / 2048
    inverse = lax.rsqrt(variance + EPSILON)
    normed = centered * inverse
    normed_ref[...] = normed
    half_ref[...] = normed.astype(BF)
    inv_ref[...] = jnp.broadcast_to(inverse, (8, 128))
    for h in range(half):
        for v in range(2):
            @pl.when(jnp.logical_not(same & (c == v)))
            def _():
                perm(v, h).wait_send()
    wcopy.wait_send()
    ag.close()
    for copy in sends + zcopies:
        copy.wait_send()


def vmem(n):
    return [pl.BlockSpec(memory_space=pltpu.VMEM)] * n


def forward(view_features, weight):
    dma = pltpu.SemaphoreType.DMA
    return pl.pallas_call(
        forward_kernel,
        out_shape=(
            jax.ShapeDtypeStruct((8, 256, 1024), BF),
            jax.ShapeDtypeStruct((2048, 128), F32),
            jax.ShapeDtypeStruct((2048, 128), BF),
            jax.ShapeDtypeStruct((8, 128), F32),
        ),
        in_specs=vmem(2),
        out_specs=tuple(vmem(4)),
        scratch_shapes=[
            pltpu.VMEM((1024, 1024), BF),
            pltpu.VMEM((4, 2, 2048, 128), BF),
            pltpu.VMEM((3, 2, 2048, 128), BF),
            pltpu.VMEM((2048, 128), BF),
            pltpu.VMEM((2048, 128), BF),
            pltpu.VMEM((2048, 128), F32),
            dma((2, NCH // 2)), dma((NCH,)), dma, dma, dma((7, NCH)), dma((7, NCH)),
            dma((3, 8)), dma((3, 8)), dma((8,)), dma((8,)),
        ],
        compiler_params=pltpu.CompilerParams(
            collective_id=0, has_side_effects=True, vmem_limit_bytes=60 * 2**20
        ),
    )(view_features, weight)


def per_device(view_features, weight, velocity):
    d, f = lax.axis_index("dp"), lax.axis_index("feat")
    p, c = d // 2, d % 2
    xg, normed, half, inverse = forward(view_features, weight)
    swap = [(i, i ^ 1) for i in range(16)]
    group = [[q * 2 + k for q in range(8)] for k in range(2)]
    other = lax.ppermute(half, "dp", swap)
    n = 2048
    wide = lax.all_gather(half, "dp", axis=1, tiled=True, axis_index_groups=group)
    mine = lax.dynamic_slice_in_dim(wide, p * 256, 256, 0)
    part = lax.dot_general(mine, wide, (((1,), (1,)), ((), ())), preferred_element_type=F32).astype(BF)
    gram = lax.psum(part.astype(F32), "feat").astype(BF)
    gram = lax.ppermute(gram, "dp", swap)
    kappa = 2.0 * REDUNDANCY / (n * n)
    grads = (kappa * jnp.dot(gram, wide, preferred_element_type=F32)).astype(BF)
    grads = lax.all_to_all(grads, "dp", 1, 0, tiled=True, axis_index_groups=group).astype(F32)
    corr = jnp.sum(half.astype(F32) * other.astype(F32), 0) / n
    extra = (-2.0 * (1.0 - corr) - 2.0 * REDUNDANCY * corr) / n
    grads = grads + extra * other.astype(F32)
    mean = jnp.mean(grads, 0)
    cross = jnp.mean(grads * normed, 0)
    og = (inverse[0] * (grads - mean - normed * cross)).astype(BF)
    og = lax.all_gather(og, "dp", axis=1, tiled=True, axis_index_groups=group)
    wg = lax.dot_general(xg.reshape(2048, 1024), og, (((0,), (0,)), ((), ())), preferred_element_type=F32)
    keep = lax.dynamic_slice_in_dim(wg, c * 512, 512, 0)
    give = lax.dynamic_slice_in_dim(wg, (1 - c) * 512, 512, 0)
    wg = keep + lax.ppermute(give, "dp", swap)
    wsq, gsq = lax.psum((jnp.sum(weight * weight), jnp.sum(wg * wg)), ("dp", "feat"))
    trust = jnp.sqrt(wsq) / (jnp.sqrt(gsq) + NORM_EPSILON)
    new_velocity = MOMENTUM * velocity + trust * wg
    return weight - LEARN_RATE * new_velocity, new_velocity


def solution(mesh):
    in_specs = (P(None, "dp", "feat"), P("dp", "feat"), P("dp", "feat"))
    out_specs = (P("dp", "feat"), P("dp", "feat"))
    return jax.shard_map(
        per_device, mesh=mesh, in_specs=in_specs, out_specs=out_specs, check_vma=False
    )
```

```python
import functools

import jax
import jax.numpy as jnp
from jax import lax
from jax.experimental import pallas as pl
from jax.experimental.pallas import tpu as pltpu
from jax.sharding import PartitionSpec as P

EPSILON = 1e-05
NORM_EPSILON = 1e-06
REDUNDANCY = 0.0051
MOMENTUM = 0.9
LEARN_RATE = 0.2
MESH = pl.DeviceIdType.MESH
BF = jnp.bfloat16
F32 = jnp.float32
NCH = 4


class Place:
    def __init__(self):
        d, f = lax.axis_index("dp"), lax.axis_index("feat")
        self.d, self.f, self.p = d, f, d // 2
        self.zh, self.x, self.c = d // 8, (d // 2) % 4, d % 2
        self.zl, self.y = f // 4, f % 4

    def at(self, zh=None, x=None, c=None, zl=None, y=None):
        zh = self.zh if zh is None else zh
        x = self.x if x is None else x
        c = self.c if c is None else c
        zl = self.zl if zl is None else zl
        y = self.y if y is None else y
        return ((zh * 4 + x) * 2 + c, zl * 4 + y)


def signal(target):
    pl.semaphore_signal(
        pltpu.get_barrier_semaphore(), inc=1, device_id=target, device_id_type=MESH
    )


def remote(src, dst, send, recv, target):
    return pltpu.make_async_remote_copy(
        src_ref=src, dst_ref=dst, send_sem=send, recv_sem=recv, device_id=target, device_id_type=MESH
    )


class Gather:
    def __init__(self, q, r, device, piece, send, recv, count=NCH):
        up, down, far, other = (r + 1) % 4, (r + 3) % 4, (r + 2) % 4, 1 - q
        self.blocks = [
            other * 4 + r, q * 4 + down, q * 4 + up, q * 4 + far,
            other * 4 + down, other * 4 + up, other * 4 + far,
        ]
        mine = q * 4 + r

        def make(block, k, slot, target):
            ref = piece(block, k)
            return remote(ref, ref, send.at[slot, k], recv.at[slot, k], target)

        to_up, to_down, to_pair = device(q, up), device(q, down), device(other, r)
        self.copies = []
        for k in range(count):
            self.copies.append([
                make(mine, k, 0, to_pair),
                make(mine, k, 1, to_up),
                make(mine, k, 2, to_down),
                make(self.blocks[1], k, 3, to_up) if k % 2 == 0 else make(self.blocks[2], k, 3, to_down),
                make(self.blocks[0], k, 4, to_up),
                make(self.blocks[0], k, 5, to_down),
                make(self.blocks[3], k, 6, to_pair),
            ])

    def own(self, k):
        for slot in (0, 1, 2):
            self.copies[k][slot].start()

    def near(self, k):
        c = self.copies[k]
        c[0].wait_recv()
        c[4].start()
        c[5].start()
        c[1].wait_recv()
        c[2].wait_recv()
        c[3].start()

    def far(self, k):
        c = self.copies[k]
        c[3].wait_recv()
        c[6].start()

    def rest(self, k, slot):
        self.copies[k][slot].wait_recv()

    def close(self):
        for c in self.copies:
            for copy in c:
                copy.wait_send()


def forward_kernel(
    x_ref, w_ref, xg, normed_ref, half_ref, inv_ref,
    wf, ys, yr, zs, zr, yacc,
    perm_s, perm_r, w_s, w_r, ag_s, ag_r, rs_s, rs_r, z_s, z_r,
):
    me = Place()
    p, f, c, x, y, zh, zl = me.p, me.f, me.c, me.x, me.y, me.zh, me.zl
    same = f == p
    piece = 256 // NCH
    half = NCH // 2
    for v in range(2):
        @pl.when(jnp.logical_not(same & (c == v)))
        def _():
            signal((f * 2 + v, p))
    partners = [
        me.at(c=1 - c), me.at(y=(y + 1) % 4), me.at(y=(y + 3) % 4), me.at(zl=1 - zl),
        me.at(x=(x + 1) % 4), me.at(x=(x + 2) % 4), me.at(x=(x + 3) % 4), me.at(zh=1 - zh),
    ]
    for t in partners:
        signal(t)
    own_rows = pl.ds(pl.multiple_of(c * 512, 512), 512)
    wf[own_rows, :] = w_ref[...].astype(BF)
    pl.semaphore_wait(pltpu.get_barrier_semaphore(), len(partners) + jnp.where(same, 1, 2))

    def perm(v, h):
        src = x_ref.at[v, pl.ds(h * piece, piece)]
        dst = xg.at[p, pl.ds(pl.multiple_of((c * half + h) * piece, piece), piece)]
        return remote(src, dst, perm_s.at[v, h], perm_r.at[c * half + h], (f * 2 + v, p))

    for h in range(half):
        for v in range(2):
            here = same & (c == v)

            @pl.when(here)
            def _():
                pltpu.make_async_copy(
                    x_ref.at[v, pl.ds(h * piece, piece)],
                    xg.at[p, pl.ds(pl.multiple_of((c * half + h) * piece, piece), piece)],
                    perm_r.at[c * half + h],
                ).start()

            @pl.when(jnp.logical_not(here))
            def _():
                perm(v, h).start()

    wcopy = remote(wf.at[own_rows], wf.at[own_rows], w_s, w_r, me.at(c=1 - c))
    wcopy.start()

    ag = Gather(
        zl, y, lambda q, r: me.at(zl=q, y=r),
        lambda b, k: xg.at[b, pl.ds(k * piece, piece)], ag_s, ag_r,
    )
    for k in (0, 2, 1, 3):
        ref = xg.at[f, pl.ds(k * piece, piece)]
        pltpu.make_async_copy(ref, ref, perm_r.at[k]).wait()
        ag.own(k)
    wcopy.wait_recv()

    order = [f] + ag.blocks
    sends = []

    def product(o):
        b = order[o]

        @pl.loop(0, 4)
        def _(j):
            cols = pl.ds(pl.multiple_of(j * 256, 256), 256)
            part = jnp.dot(xg[b], wf[:, cols], preferred_element_type=F32).astype(BF)
            rows = pl.ds(pl.multiple_of(b * 256, 256), 256)
            ys[2 * (j % 2), j // 2, rows, :] = part[:, :128]
            ys[2 * (j % 2) + 1, j // 2, rows, :] = part[:, 128:]

        rows = pl.ds(pl.multiple_of(b * 256, 256), 256)
        for dx in (2, 1, 3):
            xt = (x + dx) % 4
            copy = remote(
                ys.at[xt, :, rows], yr.at[dx - 1, :, rows], rs_s.at[dx - 1, o], rs_r.at[dx - 1, o], me.at(x=xt)
            )
            copy.start()
            sends.append(copy)

    product(0)
    for k in (0, 2, 1, 3):
        ag.near(k)
    product(1)
    product(2)
    product(3)
    for k in range(NCH):
        ag.far(k)
    product(4)
    for k in range(NCH):
        ag.rest(k, 4)
    product(5)
    for k in range(NCH):
        ag.rest(k, 5)
    product(6)
    for k in range(NCH):
        ag.rest(k, 6)
    product(7)
    zcopies = []
    for o in range(8):
        rows = pl.ds(pl.multiple_of(order[o] * 256, 256), 256)
        for copy in sends[3 * o:3 * o + 3]:
            copy.wait_recv()

        def total(side):
            s = ys[x, side, rows, :].astype(F32)
            for i in range(3):
                s = s + yr[i, side, rows, :].astype(F32)
            return s

        zs[rows, :] = total(1 - zh).astype(BF)
        copy = remote(zs.at[rows], zr.at[rows], z_s.at[o], z_r.at[o], me.at(zh=1 - zh))
        copy.start()
        zcopies.append(copy)
        yacc[rows, :] = total(zh)
    for copy in zcopies:
        copy.wait_recv()
    outputs = yacc[...] + zr[...].astype(F32)
    average = jnp.sum(outputs, 0, keepdims=True) / 2048
    centered = outputs - average
    variance = jnp.sum(centered * centered, 0, keepdims=True) / 2048
    inverse = lax.rsqrt(variance + EPSILON)
    normed = centered * inverse
    normed_ref[...] = normed
    half_ref[...] = normed.astype(BF)
    inv_ref[...] = jnp.broadcast_to(inverse, (8, 128))
    for h in range(half):
        for v in range(2):
            @pl.when(jnp.logical_not(same & (c == v)))
            def _():
                perm(v, h).wait_send()
    wcopy.wait_send()
    ag.close()
    for copy in sends + zcopies:
        copy.wait_send()


def vmem(n):
    return [pl.BlockSpec(memory_space=pltpu.VMEM)] * n


def forward(view_features, weight):
    dma = pltpu.SemaphoreType.DMA
    return pl.pallas_call(
        forward_kernel,
        out_shape=(
            jax.ShapeDtypeStruct((8, 256, 1024), BF),
            jax.ShapeDtypeStruct((2048, 128), F32),
            jax.ShapeDtypeStruct((2048, 128), BF),
            jax.ShapeDtypeStruct((8, 128), F32),
        ),
        in_specs=vmem(2),
        out_specs=tuple(vmem(4)),
        scratch_shapes=[
            pltpu.VMEM((1024, 1024), BF),
            pltpu.VMEM((4, 2, 2048, 128), BF),
            pltpu.VMEM((3, 2, 2048, 128), BF),
            pltpu.VMEM((2048, 128), BF),
            pltpu.VMEM((2048, 128), BF),
            pltpu.VMEM((2048, 128), F32),
            dma((2, NCH // 2)), dma((NCH,)), dma, dma, dma((7, NCH)), dma((7, NCH)),
            dma((3, 8)), dma((3, 8)), dma((8,)), dma((8,)),
        ],
        compiler_params=pltpu.CompilerParams(
            collective_id=0, has_side_effects=True, vmem_limit_bytes=60 * 2**20
        ),
    )(view_features, weight)


def aligned(i, size):
    return pl.ds(pl.multiple_of(i * size, size), size)


def backward_kernel(
    xg, normed_ref, half_ref, inv_ref, w_ref, wg_ref, trust_ref,
    hg, hother, gs, gr, zs, zr, gram, ts, tr, og, wacc, wrecv, msg, got, mid, got2,
    c_s, c_r, h_s, h_r, g_s, g_r, z_s, z_r, gg_s, gg_r, t_s, t_r, o_s, o_r, w_s, w_r, n_s, n_r, m_s, m_r,
):
    me = Place()
    d, p, f, c, x, y, zh, zl = me.d, me.p, me.f, me.c, me.x, me.y, me.zh, me.zl
    n = 2048
    partners = [((d + i) % 16, f) for i in range(1, 16)]
    partners += [(d, (f + i) % 8) for i in range(1, 8)]
    partners += [me.at(c=1 - c, y=(y + i) % 4) for i in range(1, 4)]
    for t in partners:
        signal(t)
    hg[:, aligned(p, 128)] = half_ref[...]
    pl.semaphore_wait(pltpu.get_barrier_semaphore(), len(partners))

    def over_dp(q, r):
        return me.at(zh=q, x=r)

    ag = Gather(zh, x, over_dp, lambda b, k: hg.at[pl.ds(k * 512, 512), aligned(b, 128)], h_s, h_r)
    for k in range(NCH):
        ag.own(k)
    swap = remote(half_ref, hother, c_s, c_r, me.at(c=1 - c))
    swap.start()
    squares = jnp.sum(w_ref[...] * w_ref[...], 0, keepdims=True)
    for k in range(NCH):
        ag.near(k)
    for k in range(NCH):
        ag.far(k)
    for k in range(NCH):
        for slot in (4, 5, 6):
            ag.rest(k, slot)

    gcopies = []
    for dy in (2, 1, 3, 0):
        yt = (y + dy) % 4
        for side in range(2):
            gs[yt, side] = lax.dot_general(
                hg[aligned(p, 256), :], hg[aligned(side * 4 + yt, 256), :],
                (((1,), (1,)), ((), ())), preferred_element_type=F32,
            ).astype(BF)
        copy = remote(gs.at[yt], gr.at[dy], g_s.at[dy], g_r.at[dy], me.at(c=1 - c, y=yt))
        copy.start()
        gcopies.append(copy)
    swap.wait_recv()
    corr = jnp.sum(half_ref[...].astype(F32) * hother[...].astype(F32), 0, keepdims=True) / n
    extra = (-2.0 * (1.0 - corr) - 2.0 * REDUNDANCY * corr) / n
    for copy in gcopies:
        copy.wait_recv()

    def total(side):
        s = gr[0, side].astype(F32)
        for i in range(1, 4):
            s = s + gr[i, side].astype(F32)
        return s

    zs[...] = total(1 - zl).astype(BF)
    zcopy = remote(zs, zr, z_s, z_r, me.at(zl=1 - zl))
    zcopy.start()
    keep = total(zl)
    zcopy.wait_recv()
    gram[:, aligned(f, 256)] = (keep + zr[...].astype(F32)).astype(BF)
    gg = Gather(
        zl, y, lambda q, r: me.at(zl=q, y=r),
        lambda b, k: gram.at[pl.ds(k * 128, 128), aligned(b, 256)], gg_s, gg_r, 2,
    )
    for k in range(2):
        gg.own(k)
    for k in range(2):
        gg.near(k)
    for k in range(2):
        gg.far(k)
    for k in range(2):
        for slot in (4, 5, 6):
            gg.rest(k, slot)

    kappa = 2.0 * REDUNDANCY / (n * n)
    for j in range(4):
        part = kappa * jnp.dot(gram[...], hg[:, pl.ds(j * 256, 256)], preferred_element_type=F32)
        ts[2 * j] = part[:, :128].astype(BF)
        ts[2 * j + 1] = part[:, 128:].astype(BF)
    tcopies = []
    for i in (2, 6, 5, 4, 3, 1, 7):
        pt = (p + i) % 8
        copy = remote(
            ts.at[pt], tr.at[aligned(p, 256)], t_s.at[i - 1], t_r.at[i - 1], (pt * 2 + c, f)
        )
        copy.start()
        tcopies.append(copy)
    tr[aligned(p, 256), :] = ts[p]
    for copy in tcopies:
        copy.wait_recv()
    grads = tr[...].astype(F32) + extra * hother[...].astype(F32)
    normed = normed_ref[...]
    mean = jnp.sum(grads, 0, keepdims=True) / n
    cross = jnp.sum(grads * normed, 0, keepdims=True) / n
    og[:, aligned(p, 128)] = (inv_ref[0:1, :] * (grads - mean - normed * cross)).astype(BF)

    oo = Gather(zh, x, over_dp, lambda b, k: og.at[pl.ds(k * 512, 512), aligned(b, 128)], o_s, o_r)
    for k in range(NCH):
        oo.own(k)
    for k in range(NCH):
        oo.near(k)
    for k in range(NCH):
        oo.far(k)
    wcopy = remote(wacc.at[aligned(1 - c, 512)], wrecv, w_s, w_r, me.at(c=1 - c))
    for k in range(NCH):
        for slot in (4, 5, 6):
            oo.rest(k, slot)
        rows = pl.ds(k * 512, 512)
        for side in range(2):
            core = (1 - c) if side == 0 else c

            @pl.loop(0, 2)
            def _(m):
                cols = aligned(core * 2 + m, 256)
                part = lax.dot_general(
                    xg[rows, cols], og[rows, :], (((0,), (0,)), ((), ())), preferred_element_type=F32
                )
                if k == 0:
                    wacc[cols, :] = part
                else:
                    wacc[cols, :] += part

            if k == NCH - 1 and side == 0:
                wcopy.start()
    wcopy.wait_recv()
    wg = wacc[aligned(c, 512), :] + wrecv[...]
    wg_ref[...] = wg
    grad_squares = jnp.sum(wg * wg, 0, keepdims=True)

    def fold(v):
        s = v[:, :128]
        for i in range(1, 8):
            s = s + v[:, i * 128:(i + 1) * 128]
        return s

    msg[...] = jnp.zeros_like(msg)
    msg[0:1, :] = fold(grad_squares)
    msg[1:2, :] = fold(squares)
    ncopies = []
    for i in range(1, 16):
        copy = remote(msg, got.at[i - 1], n_s.at[i - 1], n_r.at[i - 1], ((d + i) % 16, f))
        copy.start()
        ncopies.append(copy)
    s = msg[...]
    for i, copy in enumerate(ncopies):
        copy.wait_recv()
        s = s + got[i]
    mid[...] = s
    mcopies = []
    for i in range(1, 8):
        copy = remote(mid, got2.at[i - 1], m_s.at[i - 1], m_r.at[i - 1], (d, (f + i) % 8))
        copy.start()
        mcopies.append(copy)
    for i, copy in enumerate(mcopies):
        copy.wait_recv()
        s = s + got2[i]
    sums = jnp.sqrt(jnp.sum(s, 1, keepdims=True))
    trust_ref[...] = jnp.broadcast_to(sums[1:2, :] / (sums[0:1, :] + NORM_EPSILON), (8, 128))
    for copy in [swap, zcopy, wcopy] + gcopies + tcopies + ncopies + mcopies:
        copy.wait_send()
    for g in (ag, gg, oo):
        g.close()


def backward(xg, normed, half, inverse, weight):
    dma = pltpu.SemaphoreType.DMA
    return pl.pallas_call(
        backward_kernel,
        out_shape=(
            jax.ShapeDtypeStruct((512, 1024), F32),
            jax.ShapeDtypeStruct((8, 128), F32),
        ),
        in_specs=vmem(5),
        out_specs=tuple(vmem(2)),
        scratch_shapes=[
            pltpu.VMEM((2048, 1024), BF),
            pltpu.VMEM((2048, 128), BF),
            pltpu.VMEM((4, 2, 256, 256), BF),
            pltpu.VMEM((4, 2, 256, 256), BF),
            pltpu.VMEM((256, 256), BF),
            pltpu.VMEM((256, 256), BF),
            pltpu.VMEM((256, 2048), BF),
            pltpu.VMEM((8, 256, 128), BF),
            pltpu.VMEM((2048, 128), BF),
            pltpu.VMEM((2048, 1024), BF),
            pltpu.VMEM((1024, 1024), F32),
            pltpu.VMEM((512, 1024), F32),
            pltpu.VMEM((8, 128), F32),
            pltpu.VMEM((15, 8, 128), F32),
            pltpu.VMEM((8, 128), F32),
            pltpu.VMEM((7, 8, 128), F32),
            dma, dma, dma((7, NCH)), dma((7, NCH)), dma((4,)), dma((4,)), dma, dma,
            dma((7, 2)), dma((7, 2)), dma((7,)), dma((7,)), dma((7, NCH)), dma((7, NCH)),
            dma, dma, dma((15,)), dma((15,)), dma((7,)), dma((7,)),
        ],
        compiler_params=pltpu.CompilerParams(
            collective_id=1, has_side_effects=True, vmem_limit_bytes=60 * 2**20
        ),
    )(xg.reshape(2048, 1024), normed, half, inverse, weight)


def per_device(view_features, weight, velocity):
    xg, normed, half, inverse = forward(view_features, weight)
    wg, trust = backward(xg, normed, half, inverse, weight)
    new_velocity = MOMENTUM * velocity + trust[0:1, 0:1] * wg
    return weight - LEARN_RATE * new_velocity, new_velocity


def solution(mesh):
    in_specs = (P(None, "dp", "feat"), P("dp", "feat"), P("dp", "feat"))
    out_specs = (P("dp", "feat"), P("dp", "feat"))
    return jax.shard_map(
        per_device, mesh=mesh, in_specs=in_specs, out_specs=out_specs, check_vma=False
    )
```

```python
import functools

import jax
import jax.numpy as jnp
from jax import lax
from jax.experimental import pallas as pl
from jax.experimental.pallas import tpu as pltpu
from jax.sharding import PartitionSpec as P

EPSILON = 1e-05
NORM_EPSILON = 1e-06
REDUNDANCY = 0.0051
MOMENTUM = 0.9
LEARN_RATE = 0.2
MESH = pl.DeviceIdType.MESH
BF = jnp.bfloat16
F32 = jnp.float32
NCH = 4


class Place:
    def __init__(self):
        d, f = lax.axis_index("dp"), lax.axis_index("feat")
        self.d, self.f, self.p = d, f, d // 2
        self.zh, self.x, self.c = d // 8, (d // 2) % 4, d % 2
        self.zl, self.y = f // 4, f % 4

    def at(self, zh=None, x=None, c=None, zl=None, y=None):
        zh = self.zh if zh is None else zh
        x = self.x if x is None else x
        c = self.c if c is None else c
        zl = self.zl if zl is None else zl
        y = self.y if y is None else y
        return ((zh * 4 + x) * 2 + c, zl * 4 + y)

    def along(self, i):
        zero = self.c == 0
        return (jnp.where(zero, i * 2, self.d), jnp.where(zero, self.f, i))

    def across(self, i):
        zero = self.c == 0
        return (jnp.where(zero, self.d, i * 2 + 1), jnp.where(zero, i, self.f))

    def across_swapped(self, i):
        zero = self.c == 0
        return (jnp.where(zero, self.d + 1, i * 2), jnp.where(zero, i, self.f))


def signal(target):
    pl.semaphore_signal(
        pltpu.get_barrier_semaphore(), inc=1, device_id=target, device_id_type=MESH
    )


def remote(src, dst, send, recv, target):
    return pltpu.make_async_remote_copy(
        src_ref=src, dst_ref=dst, send_sem=send, recv_sem=recv, device_id=target, device_id_type=MESH
    )


class Gather:
    def __init__(self, q, r, device, piece, send, recv, count=NCH, paired=range(NCH)):
        up, down, far, other = (r + 1) % 4, (r + 3) % 4, (r + 2) % 4, 1 - q
        self.blocks = [
            other * 4 + r, q * 4 + down, q * 4 + up, q * 4 + far,
            other * 4 + down, other * 4 + up, other * 4 + far,
        ]
        mine = q * 4 + r
        self.paired = paired
        self.count = count

        def make(block, k, slot, target):
            ref = piece(block, k)
            return remote(ref, ref, send.at[slot, k], recv.at[slot, k], target)

        to_up, to_down, to_pair = device(q, up), device(q, down), device(other, r)
        self.copies = []
        for k in range(count):
            if k in paired:
                last = make(self.blocks[3], k, 6, to_pair)
            elif k % 2 == 0:
                last = make(self.blocks[4], k, 6, to_up)
            else:
                last = make(self.blocks[5], k, 6, to_down)
            self.copies.append([
                make(mine, k, 0, to_pair),
                make(mine, k, 1, to_up),
                make(mine, k, 2, to_down),
                make(self.blocks[1], k, 3, to_up) if k % 2 == 0 else make(self.blocks[2], k, 3, to_down),
                make(self.blocks[0], k, 4, to_up),
                make(self.blocks[0], k, 5, to_down),
                last,
            ])

    def own(self, k):
        for slot in (0, 1, 2):
            self.copies[k][slot].start()

    def near(self, k):
        c = self.copies[k]
        first = 1 + k % 2
        c[first].wait_recv()
        c[3].start()
        c[0].wait_recv()
        c[4].start()
        c[5].start()
        c[3 - first].wait_recv()

    def far(self, k):
        c = self.copies[k]
        if k in self.paired:
            c[3].wait_recv()
            c[6].start()

    def rest(self, k):
        c = self.copies[k]
        if k not in self.paired:
            c[4 + k % 2].wait_recv()
            c[6].start()
            c[3].wait_recv()
            c[5 - k % 2].wait_recv()
        else:
            c[4].wait_recv()
            c[5].wait_recv()

    def last(self, k):
        self.copies[k][6].wait_recv()

    def run(self):
        for step in (self.own, self.near, self.far, self.rest, self.last):
            for k in range(self.count):
                step(k)

    def close(self):
        for c in self.copies:
            for copy in c:
                copy.wait_send()


def aligned(i, size):
    return pl.ds(pl.multiple_of(i * size, size), size)


def kernel(
    x_ref, w_ref, wg_ref, trust_ref,
    st, xg, wf, ys, yr, zs, zr, yacc, normed_ref, half_ref,
    hg, hother, gs, gr, gzs, gzr, gram, ts, tr, og, wacc, wrecv, msg, got, mid, got2,
    p1_s, p1_r, p2_s, p2_r, v_s, v_r, ag_s, ag_r, rs_s, rs_r, z_s, z_r,
    c_s, c_r, h_s, h_r, g_s, g_r, gz_s, gz_r, gg_s, gg_r, t_s, t_r, o_s, o_r, w_s, w_r, n_s, n_r, m_s, m_r,
):
    me = Place()
    d, p, f, c, x, y, zh, zl = me.d, me.p, me.f, me.c, me.x, me.y, me.zh, me.zl
    n = 2048
    still = zh == zl
    partners = [((d + i) % 16, f) for i in range(1, 16)]
    partners += [(d, (f + i) % 8) for i in range(1, 8)]
    partners += [me.at(c=1 - c, y=(y + i) % 4) for i in range(1, 4)]
    partners += [me.at(zh=zl, x=(x + i) % 4, zl=zh) for i in range(1, 4)]
    mirror = me.at(zh=zl, zl=zh)
    for t in partners:
        signal(t)

    @pl.when(jnp.logical_not(still))
    def _():
        signal(mirror)

    pl.semaphore_wait(pltpu.get_barrier_semaphore(), len(partners) + jnp.where(still, 0, 1))

    phase1 = []
    for dj in (2, 1, 3, 0):
        for dv in (0, 1):
            v, j = (c + dv) % 2, (y + dj) % 4
            src = x_ref.at[v, aligned(j, 32)]
            dst = st.at[y, aligned(c, 32)]
            if dj == 0 and dv == 0:
                own = pltpu.make_async_copy(src, dst, p1_r.at[0, 0])
                own.start()
            else:
                copy = remote(src, dst, p1_s.at[dj, dv], p1_r.at[dj, dv], me.at(c=v, y=j))
                copy.start()
                phase1.append((dj, dv, copy))
    own_rows = aligned(c, 512)
    wf[own_rows, :] = w_ref[...].astype(BF)
    wcopy = remote(wf.at[own_rows], wf.at[own_rows], v_s, v_r, me.at(c=1 - c))
    wcopy.start()
    for dj, dv, copy in phase1:
        copy.wait_recv()
    own.wait()

    landing = pl.ds(pl.multiple_of((zh * 4 + y) * 256 + x * 64, 64), 64)
    phase2 = []
    for dx in (2, 1, 3, 0):
        xt = (x + dx) % 4
        phase2.append(remote(
            st.at[xt], xg.at[landing], p2_s.at[dx], p2_r.at[x], me.at(zh=zl, x=xt, zl=zh)
        ))
        if dx == 0:
            @pl.when(still)
            def _():
                pltpu.make_async_copy(st.at[x], xg.at[landing], p2_r.at[x]).start()

            @pl.when(jnp.logical_not(still))
            def _():
                phase2[-1].start()
        else:
            phase2[-1].start()

    ag = Gather(
        zl, y, lambda q, r: me.at(zl=q, y=r),
        lambda b, k: xg.at[pl.ds(pl.multiple_of(b * 256 + k * 64, 64), 64)], ag_s, ag_r,
    )
    for k in range(NCH):
        ref = xg.at[pl.ds(pl.multiple_of(f * 256 + k * 64, 64), 64)]
        pltpu.make_async_copy(ref, ref, p2_r.at[k]).wait()
        ag.own(k)
    wcopy.wait_recv()

    order = [f] + ag.blocks
    sends = []

    def product(o):
        rows = aligned(order[o], 256)

        @pl.loop(0, 4)
        def _(j):
            part = jnp.dot(xg[rows, :], wf[:, aligned(j, 256)], preferred_element_type=F32).astype(BF)
            ys[2 * (j % 2), j // 2, rows, :] = part[:, :128]
            ys[2 * (j % 2) + 1, j // 2, rows, :] = part[:, 128:]

        for dx in (2, 1, 3):
            xt = (x + dx) % 4
            copy = remote(
                ys.at[xt, :, rows], yr.at[dx - 1, :, rows], rs_s.at[dx - 1, o], rs_r.at[dx - 1, o], me.at(x=xt)
            )
            copy.start()
            sends.append(copy)

    product(0)
    for k in range(NCH):
        ag.near(k)
    product(1)
    product(2)
    product(3)
    for k in range(NCH):
        ag.far(k)
    product(4)
    for k in range(NCH):
        ag.rest(k)
    product(5)
    product(6)
    for k in range(NCH):
        ag.last(k)
    product(7)
    zcopies = []
    for o in range(8):
        rows = aligned(order[o], 256)
        for copy in sends[3 * o:3 * o + 3]:
            copy.wait_recv()

        def total(side):
            s = ys[x, side, rows, :].astype(F32)
            for i in range(3):
                s = s + yr[i, side, rows, :].astype(F32)
            return s

        zs[rows, :] = total(1 - zh).astype(BF)
        copy = remote(zs.at[rows], zr.at[rows], z_s.at[o], z_r.at[o], me.at(zh=1 - zh))
        copy.start()
        zcopies.append(copy)
        yacc[rows, :] = total(zh)
    for copy in zcopies:
        copy.wait_recv()
    outputs = yacc[...] + zr[...].astype(F32)
    average = jnp.sum(outputs, 0, keepdims=True) / n
    centered = outputs - average
    variance = jnp.sum(centered * centered, 0, keepdims=True) / n
    inverse = lax.rsqrt(variance + EPSILON)
    normed = centered * inverse
    normed_ref[...] = normed
    half_ref[...] = normed.astype(BF)

    mine, crossing = jnp.where(c == 0, p, f), jnp.where(c == 0, f, p)
    hg[:, aligned(mine, 128)] = normed.astype(BF)
    hh = Gather(
        mine // 4, mine % 4, lambda q, r: me.along(q * 4 + r),
        lambda b, k: hg.at[pl.ds(k * 512, 512), aligned(b, 128)], h_s, h_r, NCH, (1,),
    )
    for k in range(NCH):
        hh.own(k)
    swap = remote(half_ref, hother, c_s, c_r, me.at(c=1 - c))
    swap.start()
    squares = jnp.sum(w_ref[...] * w_ref[...], 0, keepdims=True)
    for step in (hh.near, hh.far, hh.rest, hh.last):
        for k in range(NCH):
            step(k)

    gcopies = []
    for i in (2, 1, 3, 0):
        t = (crossing + i) % 4
        for side in range(2):
            gs[t, side] = lax.dot_general(
                hg[aligned(side * 4 + t, 256), :], hg[aligned(mine, 256), :],
                (((1,), (1,)), ((), ())), preferred_element_type=F32,
            ).astype(BF)
        copy = remote(
            gs.at[t], gr.at[i], g_s.at[i], g_r.at[i], me.across_swapped((crossing // 4) * 4 + t)
        )
        copy.start()
        gcopies.append(copy)
    swap.wait_recv()
    corr = jnp.sum(half_ref[...].astype(F32) * hother[...].astype(F32), 0, keepdims=True) / n
    extra = (-2.0 * (1.0 - corr) - 2.0 * REDUNDANCY * corr) / n
    for copy in gcopies:
        copy.wait_recv()
    q = mine // 4

    def gram_total(side):
        s = gr[0, side].astype(F32)
        for i in range(1, 4):
            s = s + gr[i, side].astype(F32)
        return s

    gzs[...] = gram_total(1 - q).astype(BF)
    gzcopy = remote(gzs, gzr, gz_s, gz_r, me.along((1 - q) * 4 + mine % 4))
    gzcopy.start()
    keep = gram_total(q)
    gzcopy.wait_recv()
    gram[:, aligned(crossing, 256)] = (keep + gzr[...].astype(F32)).astype(BF)
    gg = Gather(
        crossing // 4, crossing % 4, lambda q, r: me.across(q * 4 + r),
        lambda b, k: gram.at[pl.ds(k * 128, 128), aligned(b, 256)], gg_s, gg_r, 2, (),
    )
    gg.run()

    kappa = 2.0 * REDUNDANCY / (n * n)
    for j in range(4):
        part = kappa * jnp.dot(gram[...], hg[:, pl.ds(j * 256, 256)], preferred_element_type=F32)
        ts[2 * j] = part[:, :128].astype(BF)
        ts[2 * j + 1] = part[:, 128:].astype(BF)
    tcopies = []
    for i in (2, 6, 5, 4, 3, 1, 7):
        to = (mine + i) % 8
        copy = remote(
            ts.at[to], tr.at[aligned(mine, 256)], t_s.at[i - 1], t_r.at[i - 1], me.along(to)
        )
        copy.start()
        tcopies.append(copy)
    tr[aligned(mine, 256), :] = ts[mine]
    for copy in tcopies:
        copy.wait_recv()
    grads = tr[...].astype(F32) + extra * hother[...].astype(F32)
    normed = normed_ref[...]
    mean = jnp.sum(grads, 0, keepdims=True) / n
    cross = jnp.sum(grads * normed, 0, keepdims=True) / n
    og[:, aligned(p, 128)] = (inverse * (grads - mean - normed * cross)).astype(BF)

    oo = Gather(
        zh, x, lambda q, r: me.at(zh=q, x=r),
        lambda b, k: og.at[pl.ds(k * 512, 512), aligned(b, 128)], o_s, o_r,
    )
    for step in (oo.own, oo.near, oo.far):
        for k in range(NCH):
            step(k)
    gcopy = remote(wacc.at[aligned(1 - c, 512)], wrecv, w_s, w_r, me.at(c=1 - c))
    for k in range(NCH):
        oo.rest(k)
        oo.last(k)
        rows = pl.ds(k * 512, 512)
        for side in range(2):
            core = (1 - c) if side == 0 else c

            @pl.loop(0, 2)
            def _(m):
                cols = aligned(core * 2 + m, 256)
                part = lax.dot_general(
                    xg[rows, cols], og[rows, :], (((0,), (0,)), ((), ())), preferred_element_type=F32
                )
                if k == 0:
                    wacc[cols, :] = part
                else:
                    wacc[cols, :] += part

            if k == NCH - 1 and side == 0:
                gcopy.start()
    gcopy.wait_recv()
    wg = wacc[aligned(c, 512), :] + wrecv[...]
    wg_ref[...] = wg
    grad_squares = jnp.sum(wg * wg, 0, keepdims=True)

    def fold(v):
        s = v[:, :128]
        for i in range(1, 8):
            s = s + v[:, i * 128:(i + 1) * 128]
        return s

    msg[...] = jnp.zeros_like(msg)
    msg[0:1, :] = fold(grad_squares)
    msg[1:2, :] = fold(squares)
    ncopies = []
    for i in range(1, 16):
        copy = remote(msg, got.at[i - 1], n_s.at[i - 1], n_r.at[i - 1], ((d + i) % 16, f))
        copy.start()
        ncopies.append(copy)
    s = msg[...]
    for i, copy in enumerate(ncopies):
        copy.wait_recv()
        s = s + got[i]
    mid[...] = s
    mcopies = []
    for i in range(1, 8):
        copy = remote(mid, got2.at[i - 1], m_s.at[i - 1], m_r.at[i - 1], (d, (f + i) % 8))
        copy.start()
        mcopies.append(copy)
    for i, copy in enumerate(mcopies):
        copy.wait_recv()
        s = s + got2[i]
    sums = jnp.sqrt(jnp.sum(s, 1, keepdims=True))
    trust_ref[...] = jnp.broadcast_to(sums[1:2, :] / (sums[0:1, :] + NORM_EPSILON), (8, 128))
    for copy in [swap, gzcopy, gcopy, wcopy] + sends + zcopies + gcopies + tcopies + ncopies + mcopies:
        copy.wait_send()
    for dj, dv, copy in phase1:
        copy.wait_send()
    for copy in phase2[:3]:
        copy.wait_send()

    @pl.when(jnp.logical_not(still))
    def _():
        phase2[3].wait_send()

    for g in (ag, hh, gg, oo):
        g.close()


def vmem(n):
    return [pl.BlockSpec(memory_space=pltpu.VMEM)] * n


def gradient(view_features, weight):
    dma = pltpu.SemaphoreType.DMA

    def v(*shape, kind=BF):
        return pltpu.VMEM(shape, kind)

    def two(*shape):
        return [dma(shape) if shape else dma] * 2

    return pl.pallas_call(
        kernel,
        out_shape=(
            jax.ShapeDtypeStruct((512, 1024), F32),
            jax.ShapeDtypeStruct((8, 128), F32),
        ),
        in_specs=vmem(2),
        out_specs=tuple(vmem(2)),
        scratch_shapes=[
            v(4, 64, 1024), v(2048, 1024), v(1024, 1024), v(4, 2, 2048, 128), v(3, 2, 2048, 128),
            v(2048, 128), v(2048, 128), v(2048, 128, kind=F32), v(2048, 128, kind=F32), v(2048, 128),
            v(2048, 1024), v(2048, 128), v(4, 2, 256, 256), v(4, 2, 256, 256), v(256, 256), v(256, 256),
            v(256, 2048), v(8, 256, 128), v(2048, 128), v(2048, 1024), v(1024, 1024, kind=F32),
            v(512, 1024, kind=F32), v(8, 128, kind=F32), v(15, 8, 128, kind=F32), v(8, 128, kind=F32),
            v(7, 8, 128, kind=F32),
            *two(4, 2), *two(4), *two(), *two(7, NCH), *two(3, 8), *two(8),
            *two(), *two(7, NCH), *two(4), *two(), *two(7, 2), *two(7), *two(7, NCH), *two(), *two(15), *two(7),
        ],
        compiler_params=pltpu.CompilerParams(
            collective_id=0, has_side_effects=True, vmem_limit_bytes=60 * 2**20
        ),
    )(view_features, weight)


def update_kernel(trust_ref, wg_ref, w_ref, v_ref, nw_ref, nv_ref):
    new_velocity = MOMENTUM * v_ref[...] + trust_ref[0:1, 0:1] * wg_ref[...]
    nv_ref[...] = new_velocity
    nw_ref[...] = w_ref[...] - LEARN_RATE * new_velocity


def update(trust, wg, weight, velocity):
    block = pl.BlockSpec((128, 1024), lambda i: (i, 0))
    return pl.pallas_call(
        update_kernel,
        grid=(4,),
        out_shape=(jax.ShapeDtypeStruct((512, 1024), F32),) * 2,
        in_specs=[pl.BlockSpec((8, 128), lambda i: (0, 0)), block, block, block],
        out_specs=(block, block),
    )(trust, wg, weight, velocity)


def per_device(view_features, weight, velocity):
    wg, trust = gradient(view_features, weight)
    return update(trust, wg, weight, velocity)


def solution(mesh):
    in_specs = (P(None, "dp", "feat"), P("dp", "feat"), P("dp", "feat"))
    out_specs = (P("dp", "feat"), P("dp", "feat"))
    return jax.shard_map(
        per_device, mesh=mesh, in_specs=in_specs, out_specs=out_specs, check_vma=False
    )
```

```python
import functools

import jax
import jax.numpy as jnp
from jax import lax
from jax.experimental import pallas as pl
from jax.experimental.pallas import tpu as pltpu
from jax.sharding import PartitionSpec as P

EPSILON = 1e-05
NORM_EPSILON = 1e-06
REDUNDANCY = 0.0051
MOMENTUM = 0.9
LEARN_RATE = 0.2
MESH = pl.DeviceIdType.MESH
BF = jnp.bfloat16
F32 = jnp.float32
NCH = 4


class Place:
    def __init__(self):
        d, f = lax.axis_index("dp"), lax.axis_index("feat")
        self.d, self.f, self.p = d, f, d // 2
        self.zh, self.x, self.c = d // 8, (d // 2) % 4, d % 2
        self.zl, self.y = f // 4, f % 4

    def at(self, zh=None, x=None, c=None, zl=None, y=None):
        zh = self.zh if zh is None else zh
        x = self.x if x is None else x
        c = self.c if c is None else c
        zl = self.zl if zl is None else zl
        y = self.y if y is None else y
        return ((zh * 4 + x) * 2 + c, zl * 4 + y)

    def along(self, i):
        zero = self.c == 0
        return (jnp.where(zero, i * 2, self.d), jnp.where(zero, self.f, i))

    def across(self, i):
        zero = self.c == 0
        return (jnp.where(zero, self.d, i * 2 + 1), jnp.where(zero, i, self.f))

    def across_swapped(self, i):
        zero = self.c == 0
        return (jnp.where(zero, self.d + 1, i * 2), jnp.where(zero, i, self.f))


def signal(target):
    pl.semaphore_signal(
        pltpu.get_barrier_semaphore(), inc=1, device_id=target, device_id_type=MESH
    )


def remote(src, dst, send, recv, target):
    return pltpu.make_async_remote_copy(
        src_ref=src, dst_ref=dst, send_sem=send, recv_sem=recv, device_id=target, device_id_type=MESH
    )


class Gather:
    def __init__(self, q, r, device, piece, send, recv, count=NCH, paired=range(NCH)):
        up, down, far, other = (r + 1) % 4, (r + 3) % 4, (r + 2) % 4, 1 - q
        self.blocks = [
            other * 4 + r, q * 4 + down, q * 4 + up, q * 4 + far,
            other * 4 + down, other * 4 + up, other * 4 + far,
        ]
        mine = q * 4 + r
        self.paired = paired
        self.count = count

        def make(block, k, slot, target):
            ref = piece(block, k)
            return remote(ref, ref, send.at[slot, k], recv.at[slot, k], target)

        to_up, to_down, to_pair = device(q, up), device(q, down), device(other, r)
        self.copies = []
        for k in range(count):
            if k in paired:
                last = make(self.blocks[3], k, 6, to_pair)
            elif k % 2 == 0:
                last = make(self.blocks[4], k, 6, to_up)
            else:
                last = make(self.blocks[5], k, 6, to_down)
            self.copies.append([
                make(mine, k, 0, to_pair),
                make(mine, k, 1, to_up),
                make(mine, k, 2, to_down),
                make(self.blocks[1], k, 3, to_up) if k % 2 == 0 else make(self.blocks[2], k, 3, to_down),
                make(self.blocks[0], k, 4, to_up),
                make(self.blocks[0], k, 5, to_down),
                last,
            ])

    def own(self, k):
        for slot in (0, 1, 2):
            self.copies[k][slot].start()

    def near(self, k):
        c = self.copies[k]
        first = 1 + k % 2
        c[first].wait_recv()
        c[3].start()
        c[0].wait_recv()
        c[4].start()
        c[5].start()
        c[3 - first].wait_recv()

    def far(self, k):
        c = self.copies[k]
        if k in self.paired:
            c[3].wait_recv()
            c[6].start()

    def rest(self, k):
        c = self.copies[k]
        if k not in self.paired:
            c[4 + k % 2].wait_recv()
            c[6].start()
            c[3].wait_recv()
            c[5 - k % 2].wait_recv()
        else:
            c[4].wait_recv()
            c[5].wait_recv()

    def last(self, k):
        self.copies[k][6].wait_recv()

    def run(self):
        for step in (self.own, self.near, self.far, self.rest, self.last):
            for k in range(self.count):
                step(k)

    def close(self):
        for c in self.copies:
            for copy in c:
                copy.wait_send()


def aligned(i, size):
    return pl.ds(pl.multiple_of(i * size, size), size)


def kernel(
    x_ref, w_ref, wg_ref, trust_ref,
    st, xg, wf, ys, via, yr, zs, zr, yacc, normed_ref, half_ref,
    hg, hother, gs, gr, gzs, gzr, gram, ts, tr, og, wacc, wrecv, msg, got, mid, got2,
    p1_s, p1_r, p2_s, p2_r, v_s, v_r, ag_s, ag_r, via_s, via_r, rs_s, rs_r, z_s, z_r,
    c_s, c_r, h_s, h_r, g_s, g_r, gz_s, gz_r, gg_s, gg_r, t_s, t_r, o_s, o_r, w_s, w_r, n_s, n_r, m_s, m_r,
):
    me = Place()
    d, p, f, c, x, y, zh, zl = me.d, me.p, me.f, me.c, me.x, me.y, me.zh, me.zl
    n = 2048
    still = zh == zl
    partners = [((d + i) % 16, f) for i in range(1, 16)]
    partners += [(d, (f + i) % 8) for i in range(1, 8)]
    partners += [me.at(c=1 - c, y=(y + i) % 4) for i in range(1, 4)]
    partners += [me.at(zh=zl, x=(x + i) % 4, zl=zh) for i in range(1, 4)]
    mirror = me.at(zh=zl, zl=zh)
    for t in partners:
        signal(t)

    @pl.when(jnp.logical_not(still))
    def _():
        signal(mirror)

    pl.semaphore_wait(pltpu.get_barrier_semaphore(), len(partners) + jnp.where(still, 0, 1))

    phase1, owns = [[], []], []
    for half in range(2):
        for dj in (2, 1, 3, 0):
            for dv in (0, 1):
                v, j = (c + dv) % 2, (y + dj) % 4
                src = x_ref.at[v, pl.ds(pl.multiple_of(j * 32 + half * 16, 16), 16)]
                dst = st.at[y, pl.ds(pl.multiple_of(half * 32 + c * 16, 16), 16)]
                if dj == 0 and dv == 0:
                    copy = pltpu.make_async_copy(src, dst, p1_r.at[half, 0, 0])
                    owns.append(copy)
                else:
                    copy = remote(
                        src, dst, p1_s.at[half, dj, dv], p1_r.at[half, dj, dv], me.at(c=v, y=j)
                    )
                    phase1[half].append(copy)
                copy.start()
    own_rows = aligned(c, 512)
    wf[own_rows, :] = w_ref[...].astype(BF)
    wcopy = remote(wf.at[own_rows], wf.at[own_rows], v_s, v_r, me.at(c=1 - c))
    wcopy.start()
    phase2 = [[], []]
    for half in range(2):
        for copy in phase1[half]:
            copy.wait_recv()
        owns[half].wait()
        landing = pl.ds(pl.multiple_of((zh * 4 + y) * 256 + half * 128 + x * 32, 32), 32)
        part = pl.ds(half * 32, 32)
        for dx in (2, 1, 3, 0):
            xt = (x + dx) % 4
            copy = remote(
                st.at[xt, part], xg.at[landing], p2_s.at[half, dx], p2_r.at[half, x], me.at(zh=zl, x=xt, zl=zh)
            )
            phase2[half].append(copy)
            if dx == 0:
                @pl.when(still)
                def _():
                    pltpu.make_async_copy(st.at[x, part], xg.at[landing], p2_r.at[half, x]).start()

                @pl.when(jnp.logical_not(still))
                def _():
                    copy.start()
            else:
                copy.start()

    ag = Gather(
        zl, y, lambda q, r: me.at(zl=q, y=r),
        lambda b, k: xg.at[pl.ds(pl.multiple_of(b * 256 + k * 64, 64), 64)], ag_s, ag_r,
    )
    order = [f] + ag.blocks
    up, down, far = (x + 1) % 4, (x + 3) % 4, (x + 2) % 4
    units, via_copies, ring_copies, zcopies = [], [], [], []

    def span(o, h, size=128, at=0):
        return pl.ds(pl.multiple_of(order[o] * 256 + (h * 128 + at), 64), size)

    def product(o, h):
        u = len(units)
        rows = span(o, h)

        @pl.loop(0, 4)
        def _(j):
            part = jnp.dot(xg[rows, :], wf[:, aligned(j, 256)], preferred_element_type=F32).astype(BF)
            ys[2 * (j % 2), j // 2, rows, :] = part[:, :128]
            ys[2 * (j % 2) + 1, j // 2, rows, :] = part[:, 128:]

        pair = []
        for way, to in ((0, up), (1, down)):
            copy = remote(
                ys.at[far, :, span(o, h, 64, 64 * way)], via.at[way, :, pl.ds(u * 64, 64)],
                via_s.at[way, u], via_r.at[way, u], me.at(x=to),
            )
            copy.start()
            pair.append(copy)
        units.append((o, h))
        via_copies.append(pair)

    def pass_on(u):
        o, h = units[u]
        rows = span(o, h)
        pair = []
        for way, to in ((0, up), (1, down)):
            via_copies[u][way].wait_recv()
            part = span(o, h, 64, 64 * way)
            for side in range(2):
                ys[to, side, part, :] = (
                    ys[to, side, part, :].astype(F32) + via[way, side, pl.ds(u * 64, 64), :].astype(F32)
                ).astype(BF)
            copy = remote(
                ys.at[to, :, rows], yr.at[way, :, rows], rs_s.at[way, u], rs_r.at[way, u], me.at(x=to)
            )
            copy.start()
            pair.append(copy)
        ring_copies.append(pair)

    def settle(u):
        rows = span(*units[u])
        for copy in ring_copies[u]:
            copy.wait_recv()

        def total(side):
            s = ys[x, side, rows, :].astype(F32)
            return s + yr[0, side, rows, :].astype(F32) + yr[1, side, rows, :].astype(F32)

        zs[rows, :] = total(1 - zh).astype(BF)
        copy = remote(zs.at[rows], zr.at[rows], z_s.at[u], z_r.at[u], me.at(zh=1 - zh))
        copy.start()
        zcopies.append(copy)
        yacc[rows, :] = total(zh)

    def push(o, h):
        product(o, h)
        u = len(units) - 1
        if u >= 1:
            pass_on(u - 1)
        if u >= 4:
            settle(u - 4)

    for k in range(NCH):
        for i in range(2):
            ref = xg.at[pl.ds(pl.multiple_of(f * 256 + k * 64 + i * 32, 32), 32)]
            pltpu.make_async_copy(ref, ref, p2_r.at[k // 2, 2 * (k % 2) + i]).wait()
        ag.own(k)
        if k == 1:
            wcopy.wait_recv()
            push(0, 0)
    push(0, 1)
    for h in range(2):
        for k in (2 * h, 2 * h + 1):
            ag.near(k)
        for o in (1, 2, 3):
            push(o, h)
    for step in ((0, 1), (2, 3)):
        h = step[0] // 2
        for k in step:
            ag.far(k)
        push(4, h)
        if h == 1:
            ag.last(0)
            ag.last(1)
            push(7, 0)
        for k in step:
            ag.rest(k)
        push(5, h)
        push(6, h)
    ag.last(2)
    ag.last(3)
    push(7, 1)
    pass_on(15)
    for u in range(12, 16):
        settle(u)
    for copy in zcopies:
        copy.wait_recv()
    outputs = yacc[...] + zr[...].astype(F32)
    average = jnp.sum(outputs, 0, keepdims=True) / n
    centered = outputs - average
    variance = jnp.sum(centered * centered, 0, keepdims=True) / n
    inverse = lax.rsqrt(variance + EPSILON)
    normed = centered * inverse
    normed_ref[...] = normed
    half_ref[...] = normed.astype(BF)

    mine, crossing = jnp.where(c == 0, p, f), jnp.where(c == 0, f, p)
    hg[:, aligned(mine, 128)] = normed.astype(BF)
    hh = Gather(
        mine // 4, mine % 4, lambda q, r: me.along(q * 4 + r),
        lambda b, k: hg.at[pl.ds(k * 512, 512), aligned(b, 128)], h_s, h_r, NCH, (1,),
    )
    for k in range(NCH):
        hh.own(k)
    swap = remote(half_ref, hother, c_s, c_r, me.at(c=1 - c))
    swap.start()
    squares = jnp.sum(w_ref[...] * w_ref[...], 0, keepdims=True)
    for step in (hh.near, hh.far, hh.rest, hh.last):
        for k in range(NCH):
            step(k)

    gcopies = []
    for i in (2, 1, 3, 0):
        t = (crossing + i) % 4
        for side in range(2):
            gs[t, side] = lax.dot_general(
                hg[aligned(side * 4 + t, 256), :], hg[aligned(mine, 256), :],
                (((1,), (1,)), ((), ())), preferred_element_type=F32,
            ).astype(BF)
        copy = remote(
            gs.at[t], gr.at[i], g_s.at[i], g_r.at[i], me.across_swapped((crossing // 4) * 4 + t)
        )
        copy.start()
        gcopies.append(copy)
    swap.wait_recv()
    corr = jnp.sum(half_ref[...].astype(F32) * hother[...].astype(F32), 0, keepdims=True) / n
    extra = (-2.0 * (1.0 - corr) - 2.0 * REDUNDANCY * corr) / n
    for copy in gcopies:
        copy.wait_recv()
    q = mine // 4

    def gram_total(side):
        s = gr[0, side].astype(F32)
        for i in range(1, 4):
            s = s + gr[i, side].astype(F32)
        return s

    gzs[...] = gram_total(1 - q).astype(BF)
    gzcopy = remote(gzs, gzr, gz_s, gz_r, me.along((1 - q) * 4 + mine % 4))
    gzcopy.start()
    keep = gram_total(q)
    gzcopy.wait_recv()
    gram[:, aligned(crossing, 256)] = (keep + gzr[...].astype(F32)).astype(BF)
    gg = Gather(
        crossing // 4, crossing % 4, lambda q, r: me.across(q * 4 + r),
        lambda b, k: gram.at[pl.ds(k * 128, 128), aligned(b, 256)], gg_s, gg_r, 2, (),
    )
    gg.run()

    kappa = 2.0 * REDUNDANCY / (n * n)
    tcopies = []
    member = mine % 2
    for i in (2, 1, 3, 0):
        tile = (mine // 2 + i) % 4
        part = kappa * jnp.dot(gram[...], hg[:, aligned(tile, 256)], preferred_element_type=F32)
        ts[2 * tile] = part[:, :128].astype(BF)
        ts[2 * tile + 1] = part[:, 128:].astype(BF)
        for side in range(2):
            to = 2 * tile + side
            if i == 0:
                to = mine + 1 - 2 * member
            if i != 0 or side == 0:
                copy = remote(
                    ts.at[to], tr.at[aligned(mine, 256)], t_s.at[i, side], t_r.at[i, member], me.along(to)
                )
                copy.start()
                tcopies.append(copy)
    tr[aligned(mine, 256), :] = ts[mine]
    ref = ts.at[0]
    for i in (0, 1, 2, 3):
        if i == 0:
            pltpu.make_async_copy(ref, ref, t_r.at[0, 1 - member]).wait()
        else:
            for side in range(2):
                pltpu.make_async_copy(ref, ref, t_r.at[i, side]).wait()
    grads = tr[...].astype(F32) + extra * hother[...].astype(F32)
    normed = normed_ref[...]
    mean = jnp.sum(grads, 0, keepdims=True) / n
    cross = jnp.sum(grads * normed, 0, keepdims=True) / n
    og[:, aligned(p, 128)] = (inverse * (grads - mean - normed * cross)).astype(BF)

    oo = Gather(
        zh, x, lambda q, r: me.at(zh=q, x=r),
        lambda b, k: og.at[pl.ds(k * 512, 512), aligned(b, 128)], o_s, o_r,
    )
    for step in (oo.own, oo.near, oo.far):
        for k in range(NCH):
            step(k)
    gcopy = remote(wacc.at[aligned(1 - c, 512)], wrecv, w_s, w_r, me.at(c=1 - c))
    for k in range(NCH):
        oo.rest(k)
        oo.last(k)
        rows = pl.ds(k * 512, 512)
        for side in range(2):
            core = (1 - c) if side == 0 else c

            @pl.loop(0, 2)
            def _(m):
                cols = aligned(core * 2 + m, 256)
                part = lax.dot_general(
                    xg[rows, cols], og[rows, :], (((0,), (0,)), ((), ())), preferred_element_type=F32
                )
                if k == 0:
                    wacc[cols, :] = part
                else:
                    wacc[cols, :] += part

            if k == NCH - 1 and side == 0:
                gcopy.start()
    gcopy.wait_recv()
    wg = wacc[aligned(c, 512), :] + wrecv[...]
    wg_ref[...] = wg
    grad_squares = jnp.sum(wg * wg, 0, keepdims=True)

    def fold(v):
        s = v[:, :128]
        for i in range(1, 8):
            s = s + v[:, i * 128:(i + 1) * 128]
        return s

    msg[...] = jnp.zeros_like(msg)
    msg[0:1, :] = fold(grad_squares)
    msg[1:2, :] = fold(squares)
    ncopies = []
    for i in range(1, 16):
        copy = remote(msg, got.at[i - 1], n_s.at[i - 1], n_r.at[i - 1], ((d + i) % 16, f))
        copy.start()
        ncopies.append(copy)
    s = msg[...]
    for i, copy in enumerate(ncopies):
        copy.wait_recv()
        s = s + got[i]
    mid[...] = s
    mcopies = []
    for i in range(1, 8):
        copy = remote(mid, got2.at[i - 1], m_s.at[i - 1], m_r.at[i - 1], (d, (f + i) % 8))
        copy.start()
        mcopies.append(copy)
    for i, copy in enumerate(mcopies):
        copy.wait_recv()
        s = s + got2[i]
    sums = jnp.sqrt(jnp.sum(s, 1, keepdims=True))
    trust_ref[...] = jnp.broadcast_to(sums[1:2, :] / (sums[0:1, :] + NORM_EPSILON), (8, 128))
    for copy in [swap, gzcopy, gcopy, wcopy] + sum(via_copies + ring_copies, []) + zcopies + gcopies + tcopies + ncopies + mcopies:
        copy.wait_send()
    for copy in phase1[0] + phase1[1] + phase2[0][:3] + phase2[1][:3]:
        copy.wait_send()

    @pl.when(jnp.logical_not(still))
    def _():
        phase2[0][3].wait_send()
        phase2[1][3].wait_send()

    for g in (ag, hh, gg, oo):
        g.close()


def vmem(n):
    return [pl.BlockSpec(memory_space=pltpu.VMEM)] * n


def gradient(view_features, weight):
    dma = pltpu.SemaphoreType.DMA

    def v(*shape, kind=BF):
        return pltpu.VMEM(shape, kind)

    def two(*shape):
        return [dma(shape) if shape else dma] * 2

    return pl.pallas_call(
        kernel,
        out_shape=(
            jax.ShapeDtypeStruct((512, 1024), F32),
            jax.ShapeDtypeStruct((8, 128), F32),
        ),
        in_specs=vmem(2),
        out_specs=tuple(vmem(2)),
        scratch_shapes=[
            v(4, 64, 1024), v(2048, 1024), v(1024, 1024), v(4, 2, 2048, 128), v(2, 2, 1024, 128), v(2, 2, 2048, 128),
            v(2048, 128), v(2048, 128), v(2048, 128, kind=F32), v(2048, 128, kind=F32), v(2048, 128),
            v(2048, 1024), v(2048, 128), v(4, 2, 256, 256), v(4, 2, 256, 256), v(256, 256), v(256, 256),
            v(256, 2048), v(8, 256, 128), v(2048, 128), v(2048, 1024), v(1024, 1024, kind=F32),
            v(512, 1024, kind=F32), v(8, 128, kind=F32), v(15, 8, 128, kind=F32), v(8, 128, kind=F32),
            v(7, 8, 128, kind=F32),
            *two(2, 4, 2), *two(2, 4), *two(), *two(7, NCH), *two(2, 16), *two(2, 16), *two(16),
            *two(), *two(7, NCH), *two(4), *two(), *two(7, 2), *two(4, 2), *two(7, NCH), *two(), *two(15), *two(7),
        ],
        compiler_params=pltpu.CompilerParams(
            collective_id=0, has_side_effects=True, vmem_limit_bytes=60 * 2**20
        ),
    )(view_features, weight)


def update_kernel(trust_ref, wg_ref, w_ref, v_ref, nw_ref, nv_ref):
    new_velocity = MOMENTUM * v_ref[...] + trust_ref[0:1, 0:1] * wg_ref[...]
    nv_ref[...] = new_velocity
    nw_ref[...] = w_ref[...] - LEARN_RATE * new_velocity


def update(trust, wg, weight, velocity):
    block = pl.BlockSpec((128, 1024), lambda i: (i, 0))
    return pl.pallas_call(
        update_kernel,
        grid=(4,),
        out_shape=(jax.ShapeDtypeStruct((512, 1024), F32),) * 2,
        in_specs=[pl.BlockSpec((8, 128), lambda i: (0, 0)), block, block, block],
        out_specs=(block, block),
    )(trust, wg, weight, velocity)


def per_device(view_features, weight, velocity):
    wg, trust = gradient(view_features, weight)
    return update(trust, wg, weight, velocity)


def solution(mesh):
    in_specs = (P(None, "dp", "feat"), P("dp", "feat"), P("dp", "feat"))
    out_specs = (P("dp", "feat"), P("dp", "feat"))
    return jax.shard_map(
        per_device, mesh=mesh, in_specs=in_specs, out_specs=out_specs, check_vma=False
    )
```

```python
import functools

import jax
import jax.numpy as jnp
from jax import lax
from jax.experimental import pallas as pl
from jax.experimental.pallas import tpu as pltpu
from jax.sharding import PartitionSpec as P

EPSILON = 1e-05
NORM_EPSILON = 1e-06
REDUNDANCY = 0.0051
MOMENTUM = 0.9
LEARN_RATE = 0.2
MESH = pl.DeviceIdType.MESH
BF = jnp.bfloat16
F32 = jnp.float32
NCH = 4


class Place:
    def __init__(self):
        d, f = lax.axis_index("dp"), lax.axis_index("feat")
        self.d, self.f, self.p = d, f, d // 2
        self.zh, self.x, self.c = d // 8, (d // 2) % 4, d % 2
        self.zl, self.y = f // 4, f % 4

    def at(self, zh=None, x=None, c=None, zl=None, y=None):
        zh = self.zh if zh is None else zh
        x = self.x if x is None else x
        c = self.c if c is None else c
        zl = self.zl if zl is None else zl
        y = self.y if y is None else y
        return ((zh * 4 + x) * 2 + c, zl * 4 + y)

    def along(self, i):
        zero = self.c == 0
        return (jnp.where(zero, i * 2, self.d), jnp.where(zero, self.f, i))

    def across(self, i):
        zero = self.c == 0
        return (jnp.where(zero, self.d, i * 2 + 1), jnp.where(zero, i, self.f))

    def across_swapped(self, i):
        zero = self.c == 0
        return (jnp.where(zero, self.d + 1, i * 2), jnp.where(zero, i, self.f))


def signal(target):
    pl.semaphore_signal(
        pltpu.get_barrier_semaphore(), inc=1, device_id=target, device_id_type=MESH
    )


def remote(src, dst, send, recv, target):
    return pltpu.make_async_remote_copy(
        src_ref=src, dst_ref=dst, send_sem=send, recv_sem=recv, device_id=target, device_id_type=MESH
    )


class Gather:
    def __init__(self, q, r, device, piece, send, recv, count=NCH, paired=range(NCH)):
        up, down, far, other = (r + 1) % 4, (r + 3) % 4, (r + 2) % 4, 1 - q
        self.blocks = [
            other * 4 + r, q * 4 + down, q * 4 + up, q * 4 + far,
            other * 4 + down, other * 4 + up, other * 4 + far,
        ]
        mine = q * 4 + r
        self.paired = paired
        self.count = count

        def make(block, k, slot, target):
            ref = piece(block, k)
            return remote(ref, ref, send.at[slot, k], recv.at[slot, k], target)

        to_up, to_down, to_pair = device(q, up), device(q, down), device(other, r)
        self.copies = []
        for k in range(count):
            if k in paired:
                last = make(self.blocks[3], k, 6, to_pair)
            elif k % 2 == 0:
                last = make(self.blocks[4], k, 6, to_up)
            else:
                last = make(self.blocks[5], k, 6, to_down)
            self.copies.append([
                make(mine, k, 0, to_pair),
                make(mine, k, 1, to_up),
                make(mine, k, 2, to_down),
                make(self.blocks[1], k, 3, to_up) if k % 2 == 0 else make(self.blocks[2], k, 3, to_down),
                make(self.blocks[0], k, 4, to_up),
                make(self.blocks[0], k, 5, to_down),
                last,
            ])

    def own(self, k):
        for slot in (0, 1, 2):
            self.copies[k][slot].start()

    def near(self, k):
        c = self.copies[k]
        first = 1 + k % 2
        c[first].wait_recv()
        c[3].start()
        c[3 - first].wait_recv()

    def turn(self, k):
        c = self.copies[k]
        c[0].wait_recv()
        c[4].start()
        c[5].start()

    def far(self, k):
        c = self.copies[k]
        if k in self.paired:
            c[3].wait_recv()
            c[6].start()

    def rest(self, k):
        c = self.copies[k]
        if k not in self.paired:
            c[4 + k % 2].wait_recv()
            c[6].start()
            c[3].wait_recv()
            c[5 - k % 2].wait_recv()
        else:
            c[4].wait_recv()
            c[5].wait_recv()

    def last(self, k):
        self.copies[k][6].wait_recv()

    def run(self):
        for step in (self.own, self.near, self.turn, self.far, self.rest, self.last):
            for k in range(self.count):
                step(k)

    def close(self):
        for c in self.copies:
            for copy in c:
                copy.wait_send()


def aligned(i, size):
    return pl.ds(pl.multiple_of(i * size, size), size)


def kernel(
    x_ref, w_ref, wg_ref, trust_ref,
    st, xg, wf, ys, via, yr, zs, zr, yacc, normed_ref, half_ref,
    hg, hother, gs, gr, gzs, gzr, gram, ts, tr, og, wacc, wrecv, msg, got, mid, got2,
    p1_s, p1_r, p2_s, p2_r, v_s, v_r, ag_s, ag_r, via_s, via_r, rs_s, rs_r, z_s, z_r,
    c_s, c_r, h_s, h_r, g_s, g_r, gz_s, gz_r, gg_s, gg_r, t_s, t_r, o_s, o_r, w_s, w_r, n_s, n_r, m_s, m_r,
):
    me = Place()
    d, p, f, c, x, y, zh, zl = me.d, me.p, me.f, me.c, me.x, me.y, me.zh, me.zl
    n = 2048
    still = zh == zl
    partners = [((d + i) % 16, f) for i in range(1, 16)]
    partners += [(d, (f + i) % 8) for i in range(1, 8)]
    partners += [me.at(c=1 - c, y=(y + i) % 4) for i in range(1, 4)]
    partners += [me.at(zh=zl, x=(x + i) % 4, zl=zh) for i in range(1, 4)]
    mirror = me.at(zh=zl, zl=zh)
    for t in partners:
        signal(t)

    @pl.when(jnp.logical_not(still))
    def _():
        signal(mirror)

    pl.semaphore_wait(pltpu.get_barrier_semaphore(), len(partners) + jnp.where(still, 0, 1))

    phase1, owns = [[], []], []
    for half in range(2):
        for dj in (2, 1, 3, 0):
            for dv in (0, 1):
                v, j = (c + dv) % 2, (y + dj) % 4
                src = x_ref.at[v, pl.ds(pl.multiple_of(j * 32 + half * 16, 16), 16)]
                dst = st.at[y, pl.ds(pl.multiple_of(half * 32 + c * 16, 16), 16)]
                if dj == 0 and dv == 0:
                    copy = pltpu.make_async_copy(src, dst, p1_r.at[half, 0, 0])
                    owns.append(copy)
                else:
                    copy = remote(
                        src, dst, p1_s.at[half, dj, dv], p1_r.at[half, dj, dv], me.at(c=v, y=j)
                    )
                    phase1[half].append(copy)
                copy.start()
    own_rows = aligned(c, 512)
    wf[own_rows, :] = w_ref[...].astype(BF)
    wcopy = remote(wf.at[own_rows], wf.at[own_rows], v_s, v_r, me.at(c=1 - c))
    wcopy.start()
    phase2 = [[], []]
    for half in range(2):
        for copy in phase1[half]:
            copy.wait_recv()
        owns[half].wait()
        landing = pl.ds(pl.multiple_of((zh * 4 + y) * 256 + half * 128 + x * 32, 32), 32)
        part = pl.ds(half * 32, 32)
        for dx in (2, 1, 3, 0):
            xt = (x + dx) % 4
            copy = remote(
                st.at[xt, part], xg.at[landing], p2_s.at[half, dx], p2_r.at[half, x], me.at(zh=zl, x=xt, zl=zh)
            )
            phase2[half].append(copy)
            if dx == 0:
                @pl.when(still)
                def _():
                    pltpu.make_async_copy(st.at[x, part], xg.at[landing], p2_r.at[half, x]).start()

                @pl.when(jnp.logical_not(still))
                def _():
                    copy.start()
            else:
                copy.start()

    ag = Gather(
        zl, y, lambda q, r: me.at(zl=q, y=r),
        lambda b, k: xg.at[pl.ds(pl.multiple_of(b * 256 + k * 64, 64), 64)], ag_s, ag_r,
    )
    order = [f] + ag.blocks
    up, down, far = (x + 1) % 4, (x + 3) % 4, (x + 2) % 4
    units, via_copies, ring_copies, zcopies = [], [], [], []

    def span(o, h, size=128, at=0):
        return pl.ds(pl.multiple_of(order[o] * 256 + (h * 128 + at), 64), size)

    def product(o, h):
        u = len(units)
        rows = span(o, h)

        @pl.loop(0, 4)
        def _(j):
            part = jnp.dot(xg[rows, :], wf[:, aligned(j, 256)], preferred_element_type=F32).astype(BF)
            ys[2 * (j % 2), j // 2, rows, :] = part[:, :128]
            ys[2 * (j % 2) + 1, j // 2, rows, :] = part[:, 128:]

        pair = []
        for way, to in ((0, up), (1, down)):
            copy = remote(
                ys.at[far, :, span(o, h, 64, 64 * way)], via.at[way, :, pl.ds(u * 64, 64)],
                via_s.at[way, u], via_r.at[way, u], me.at(x=to),
            )
            copy.start()
            pair.append(copy)
        units.append((o, h))
        via_copies.append(pair)

    def pass_on(u):
        o, h = units[u]
        rows = span(o, h)
        pair = []
        for way, to in ((0, up), (1, down)):
            via_copies[u][way].wait_recv()
            part = span(o, h, 64, 64 * way)
            for side in range(2):
                ys[to, side, part, :] = (
                    ys[to, side, part, :].astype(F32) + via[way, side, pl.ds(u * 64, 64), :].astype(F32)
                ).astype(BF)
            copy = remote(
                ys.at[to, :, rows], yr.at[way, :, rows], rs_s.at[way, u], rs_r.at[way, u], me.at(x=to)
            )
            copy.start()
            pair.append(copy)
        ring_copies.append(pair)

    def settle(u):
        rows = span(*units[u])
        for copy in ring_copies[u]:
            copy.wait_recv()

        def total(side):
            s = ys[x, side, rows, :].astype(F32)
            return s + yr[0, side, rows, :].astype(F32) + yr[1, side, rows, :].astype(F32)

        zs[rows, :] = total(1 - zh).astype(BF)
        copy = remote(zs.at[rows], zr.at[rows], z_s.at[u], z_r.at[u], me.at(zh=1 - zh))
        copy.start()
        zcopies.append(copy)
        yacc[rows, :] = total(zh)

    def push(o, h):
        product(o, h)
        u = len(units) - 1
        if u >= 1:
            pass_on(u - 1)
        if u >= 4:
            settle(u - 4)

    for k in range(NCH):
        for i in range(2):
            ref = xg.at[pl.ds(pl.multiple_of(f * 256 + k * 64 + i * 32, 32), 32)]
            pltpu.make_async_copy(ref, ref, p2_r.at[k // 2, 2 * (k % 2) + i]).wait()
        ag.own(k)
        if k == 1:
            wcopy.wait_recv()
            push(0, 0)
    push(0, 1)
    for h in range(2):
        for k in (2 * h, 2 * h + 1):
            ag.near(k)
            ag.turn(k)
        for o in (1, 2, 3):
            push(o, h)
    for step in ((0, 1), (2, 3)):
        h = step[0] // 2
        for k in step:
            ag.far(k)
        push(4, h)
        if h == 1:
            ag.last(0)
            ag.last(1)
            push(7, 0)
        for k in step:
            ag.rest(k)
        push(5, h)
        push(6, h)
    ag.last(2)
    ag.last(3)
    push(7, 1)
    pass_on(15)
    for u in range(12, 16):
        settle(u)
    for copy in zcopies:
        copy.wait_recv()
    outputs = yacc[...] + zr[...].astype(F32)
    average = jnp.sum(outputs, 0, keepdims=True) / n
    centered = outputs - average
    variance = jnp.sum(centered * centered, 0, keepdims=True) / n
    inverse = lax.rsqrt(variance + EPSILON)
    normed = centered * inverse
    normed_ref[...] = normed
    half_ref[...] = normed.astype(BF)

    mine, crossing = jnp.where(c == 0, p, f), jnp.where(c == 0, f, p)
    hg[:, aligned(mine, 128)] = normed.astype(BF)
    hh = Gather(
        mine // 4, mine % 4, lambda q, r: me.along(q * 4 + r),
        lambda b, k: hg.at[pl.ds(k * 512, 512), aligned(b, 128)], h_s, h_r, NCH, (1,),
    )
    for k in range(NCH):
        hh.own(k)
    swap = remote(half_ref, hother, c_s, c_r, me.at(c=1 - c))
    swap.start()
    squares = jnp.sum(w_ref[...] * w_ref[...], 0, keepdims=True)
    for step in (hh.near, hh.turn, hh.far, hh.rest, hh.last):
        for k in range(NCH):
            step(k)

    gcopies = []
    for i in (2, 1, 3, 0):
        t = (crossing + i) % 4
        for side in range(2):
            gs[t, side] = lax.dot_general(
                hg[aligned(side * 4 + t, 256), :], hg[aligned(mine, 256), :],
                (((1,), (1,)), ((), ())), preferred_element_type=F32,
            ).astype(BF)
        copy = remote(
            gs.at[t], gr.at[i], g_s.at[i], g_r.at[i], me.across_swapped((crossing // 4) * 4 + t)
        )
        copy.start()
        gcopies.append(copy)
    swap.wait_recv()
    corr = jnp.sum(half_ref[...].astype(F32) * hother[...].astype(F32), 0, keepdims=True) / n
    extra = (-2.0 * (1.0 - corr) - 2.0 * REDUNDANCY * corr) / n
    for copy in gcopies:
        copy.wait_recv()
    q = mine // 4

    def gram_total(side):
        s = gr[0, side].astype(F32)
        for i in range(1, 4):
            s = s + gr[i, side].astype(F32)
        return s

    gzs[...] = gram_total(1 - q).astype(BF)
    gzcopy = remote(gzs, gzr, gz_s, gz_r, me.along((1 - q) * 4 + mine % 4))
    gzcopy.start()
    keep = gram_total(q)
    gzcopy.wait_recv()
    gram[:, aligned(crossing, 256)] = (keep + gzr[...].astype(F32)).astype(BF)
    gg = Gather(
        crossing // 4, crossing % 4, lambda q, r: me.across(q * 4 + r),
        lambda b, k: gram.at[pl.ds(k * 128, 128), aligned(b, 256)], gg_s, gg_r, 2, (),
    )
    gg.run()

    kappa = 2.0 * REDUNDANCY / (n * n)
    tcopies = []
    member = mine % 2
    for i in (2, 1, 3, 0):
        tile = (mine // 2 + i) % 4
        part = kappa * jnp.dot(gram[...], hg[:, aligned(tile, 256)], preferred_element_type=F32)
        ts[2 * tile] = part[:, :128].astype(BF)
        ts[2 * tile + 1] = part[:, 128:].astype(BF)
        for side in range(2):
            to = 2 * tile + side
            if i == 0:
                to = mine + 1 - 2 * member
            if i != 0 or side == 0:
                copy = remote(
                    ts.at[to], tr.at[aligned(mine, 256)], t_s.at[i, side], t_r.at[i, member], me.along(to)
                )
                copy.start()
                tcopies.append(copy)
    tr[aligned(mine, 256), :] = ts[mine]
    ref = ts.at[0]
    for i in (0, 1, 2, 3):
        if i == 0:
            pltpu.make_async_copy(ref, ref, t_r.at[0, 1 - member]).wait()
        else:
            for side in range(2):
                pltpu.make_async_copy(ref, ref, t_r.at[i, side]).wait()
    grads = tr[...].astype(F32) + extra * hother[...].astype(F32)
    normed = normed_ref[...]
    mean = jnp.sum(grads, 0, keepdims=True) / n
    cross = jnp.sum(grads * normed, 0, keepdims=True) / n
    og[:, aligned(p, 128)] = (inverse * (grads - mean - normed * cross)).astype(BF)

    oo = Gather(
        zh, x, lambda q, r: me.at(zh=q, x=r),
        lambda b, k: og.at[pl.ds(k * 512, 512), aligned(b, 128)], o_s, o_r,
    )
    for step in (oo.own, oo.near, oo.turn, oo.far):
        for k in range(NCH):
            step(k)
    gcopy = remote(wacc.at[aligned(1 - c, 512)], wrecv, w_s, w_r, me.at(c=1 - c))
    for k in range(NCH):
        oo.rest(k)
        oo.last(k)
        rows = pl.ds(k * 512, 512)
        for side in range(2):
            core = (1 - c) if side == 0 else c

            @pl.loop(0, 2)
            def _(m):
                cols = aligned(core * 2 + m, 256)
                part = lax.dot_general(
                    xg[rows, cols], og[rows, :], (((0,), (0,)), ((), ())), preferred_element_type=F32
                )
                if k == 0:
                    wacc[cols, :] = part
                else:
                    wacc[cols, :] += part

            if k == NCH - 1 and side == 0:
                gcopy.start()
    gcopy.wait_recv()
    wg = wacc[aligned(c, 512), :] + wrecv[...]
    wg_ref[...] = wg
    grad_squares = jnp.sum(wg * wg, 0, keepdims=True)

    def fold(v):
        s = v[:, :128]
        for i in range(1, 8):
            s = s + v[:, i * 128:(i + 1) * 128]
        return s

    msg[...] = jnp.zeros_like(msg)
    msg[0:1, :] = fold(grad_squares)
    msg[1:2, :] = fold(squares)
    ncopies = []
    for i in range(1, 16):
        copy = remote(msg, got.at[i - 1], n_s.at[i - 1], n_r.at[i - 1], ((d + i) % 16, f))
        copy.start()
        ncopies.append(copy)
    s = msg[...]
    for i, copy in enumerate(ncopies):
        copy.wait_recv()
        s = s + got[i]
    mid[...] = s
    mcopies = []
    for i in range(1, 8):
        copy = remote(mid, got2.at[i - 1], m_s.at[i - 1], m_r.at[i - 1], (d, (f + i) % 8))
        copy.start()
        mcopies.append(copy)
    for i, copy in enumerate(mcopies):
        copy.wait_recv()
        s = s + got2[i]
    sums = jnp.sqrt(jnp.sum(s, 1, keepdims=True))
    trust_ref[...] = jnp.broadcast_to(sums[1:2, :] / (sums[0:1, :] + NORM_EPSILON), (8, 128))
    for copy in [swap, gzcopy, gcopy, wcopy] + sum(via_copies + ring_copies, []) + zcopies + gcopies + tcopies + ncopies + mcopies:
        copy.wait_send()
    for copy in phase1[0] + phase1[1] + phase2[0][:3] + phase2[1][:3]:
        copy.wait_send()

    @pl.when(jnp.logical_not(still))
    def _():
        phase2[0][3].wait_send()
        phase2[1][3].wait_send()

    for g in (ag, hh, gg, oo):
        g.close()


def vmem(n):
    return [pl.BlockSpec(memory_space=pltpu.VMEM)] * n


def gradient(view_features, weight):
    dma = pltpu.SemaphoreType.DMA

    def v(*shape, kind=BF):
        return pltpu.VMEM(shape, kind)

    def two(*shape):
        return [dma(shape) if shape else dma] * 2

    return pl.pallas_call(
        kernel,
        out_shape=(
            jax.ShapeDtypeStruct((512, 1024), F32),
            jax.ShapeDtypeStruct((8, 128), F32),
        ),
        in_specs=vmem(2),
        out_specs=tuple(vmem(2)),
        scratch_shapes=[
            v(4, 64, 1024), v(2048, 1024), v(1024, 1024), v(4, 2, 2048, 128), v(2, 2, 1024, 128), v(2, 2, 2048, 128),
            v(2048, 128), v(2048, 128), v(2048, 128, kind=F32), v(2048, 128, kind=F32), v(2048, 128),
            v(2048, 1024), v(2048, 128), v(4, 2, 256, 256), v(4, 2, 256, 256), v(256, 256), v(256, 256),
            v(256, 2048), v(8, 256, 128), v(2048, 128), v(2048, 1024), v(1024, 1024, kind=F32),
            v(512, 1024, kind=F32), v(8, 128, kind=F32), v(15, 8, 128, kind=F32), v(8, 128, kind=F32),
            v(7, 8, 128, kind=F32),
            *two(2, 4, 2), *two(2, 4), *two(), *two(7, NCH), *two(2, 16), *two(2, 16), *two(16),
            *two(), *two(7, NCH), *two(4), *two(), *two(7, 2), *two(4, 2), *two(7, NCH), *two(), *two(15), *two(7),
        ],
        compiler_params=pltpu.CompilerParams(
            collective_id=0, has_side_effects=True, vmem_limit_bytes=60 * 2**20
        ),
    )(view_features, weight)


def update_kernel(trust_ref, wg_ref, w_ref, v_ref, nw_ref, nv_ref):
    new_velocity = MOMENTUM * v_ref[...] + trust_ref[0:1, 0:1] * wg_ref[...]
    nv_ref[...] = new_velocity
    nw_ref[...] = w_ref[...] - LEARN_RATE * new_velocity


def update(trust, wg, weight, velocity):
    block = pl.BlockSpec((256, 1024), lambda i: (i, 0))
    return pl.pallas_call(
        update_kernel,
        grid=(2,),
        out_shape=(jax.ShapeDtypeStruct((512, 1024), F32),) * 2,
        in_specs=[pl.BlockSpec((8, 128), lambda i: (0, 0)), block, block, block],
        out_specs=(block, block),
    )(trust, wg, weight, velocity)


def per_device(view_features, weight, velocity):
    wg, trust = gradient(view_features, weight)
    return update(trust, wg, weight, velocity)


def solution(mesh):
    in_specs = (P(None, "dp", "feat"), P("dp", "feat"), P("dp", "feat"))
    out_specs = (P("dp", "feat"), P("dp", "feat"))
    return jax.shard_map(
        per_device, mesh=mesh, in_specs=in_specs, out_specs=out_specs, check_vma=False
    )
```

```python
import functools

import jax
import jax.numpy as jnp
from jax import lax
from jax.experimental import pallas as pl
from jax.experimental.pallas import tpu as pltpu
from jax.sharding import PartitionSpec as P

EPSILON = 1e-05
NORM_EPSILON = 1e-06
REDUNDANCY = 0.0051
MOMENTUM = 0.9
LEARN_RATE = 0.2
MESH = pl.DeviceIdType.MESH
BF = jnp.bfloat16
F32 = jnp.float32
NCH = 4


class Place:
    def __init__(self):
        d, f = lax.axis_index("dp"), lax.axis_index("feat")
        self.d, self.f, self.p = d, f, d // 2
        self.zh, self.x, self.c = d // 8, (d // 2) % 4, d % 2
        self.zl, self.y = f // 4, f % 4

    def at(self, zh=None, x=None, c=None, zl=None, y=None):
        zh = self.zh if zh is None else zh
        x = self.x if x is None else x
        c = self.c if c is None else c
        zl = self.zl if zl is None else zl
        y = self.y if y is None else y
        return ((zh * 4 + x) * 2 + c, zl * 4 + y)

    def along(self, i):
        zero = self.c == 0
        return (jnp.where(zero, i * 2, self.d), jnp.where(zero, self.f, i))

    def across(self, i):
        zero = self.c == 0
        return (jnp.where(zero, self.d, i * 2 + 1), jnp.where(zero, i, self.f))

    def across_swapped(self, i):
        zero = self.c == 0
        return (jnp.where(zero, self.d + 1, i * 2), jnp.where(zero, i, self.f))


def signal(target):
    pl.semaphore_signal(
        pltpu.get_barrier_semaphore(), inc=1, device_id=target, device_id_type=MESH
    )


def remote(src, dst, send, recv, target):
    return pltpu.make_async_remote_copy(
        src_ref=src, dst_ref=dst, send_sem=send, recv_sem=recv, device_id=target, device_id_type=MESH
    )


class Gather:
    def __init__(self, q, r, device, piece, send, recv, count=NCH, paired=range(NCH)):
        up, down, far, other = (r + 1) % 4, (r + 3) % 4, (r + 2) % 4, 1 - q
        self.blocks = [
            other * 4 + r, q * 4 + down, q * 4 + up, q * 4 + far,
            other * 4 + down, other * 4 + up, other * 4 + far,
        ]
        mine = q * 4 + r
        self.paired = paired
        self.count = count

        def make(block, k, slot, target):
            ref = piece(block, k)
            return remote(ref, ref, send.at[slot, k], recv.at[slot, k], target)

        to_up, to_down, to_pair = device(q, up), device(q, down), device(other, r)
        self.copies = []
        for k in range(count):
            if k in paired:
                last = make(self.blocks[3], k, 6, to_pair)
            elif k % 2 == 0:
                last = make(self.blocks[4], k, 6, to_up)
            else:
                last = make(self.blocks[5], k, 6, to_down)
            self.copies.append([
                make(mine, k, 0, to_pair),
                make(mine, k, 1, to_up),
                make(mine, k, 2, to_down),
                make(self.blocks[1], k, 3, to_up) if k % 2 == 0 else make(self.blocks[2], k, 3, to_down),
                make(self.blocks[0], k, 4, to_up),
                make(self.blocks[0], k, 5, to_down),
                last,
            ])

    def own(self, k):
        for slot in (0, 1, 2):
            self.copies[k][slot].start()

    def near(self, k):
        c = self.copies[k]
        first = 1 + k % 2
        c[first].wait_recv()
        c[3].start()
        c[3 - first].wait_recv()

    def turn(self, k):
        c = self.copies[k]
        c[0].wait_recv()
        c[4].start()
        c[5].start()

    def far(self, k):
        c = self.copies[k]
        if k in self.paired:
            c[3].wait_recv()
            c[6].start()

    def rest(self, k):
        c = self.copies[k]
        if k not in self.paired:
            c[4 + k % 2].wait_recv()
            c[6].start()
            c[3].wait_recv()
            c[5 - k % 2].wait_recv()
        else:
            c[4].wait_recv()
            c[5].wait_recv()

    def last(self, k):
        self.copies[k][6].wait_recv()

    def run(self):
        for step in (self.own, self.near, self.turn, self.far, self.rest, self.last):
            for k in range(self.count):
                step(k)

    def close(self):
        for c in self.copies:
            for copy in c:
                copy.wait_send()


def aligned(i, size):
    return pl.ds(pl.multiple_of(i * size, size), size)


def kernel(
    x_ref, w_ref, wg_ref, trust_ref,
    st, xg, wf, ys, via, yr, zs, zr, yacc, normed_ref, half_ref,
    hg, hother, gs, gr, gzs, gzr, gram, ts, tr, og, wacc, wrecv, msg, got, mid, got2,
    p1_s, p1_r, p2_s, p2_r, v_s, v_r, ag_s, ag_r, via_s, via_r, rs_s, rs_r, z_s, z_r,
    c_s, c_r, h_s, h_r, g_s, g_r, gz_s, gz_r, gg_s, gg_r, t_s, t_r, o_s, o_r, w_s, w_r, n_s, n_r, m_s, m_r,
):
    me = Place()
    d, p, f, c, x, y, zh, zl = me.d, me.p, me.f, me.c, me.x, me.y, me.zh, me.zl
    n = 2048
    still = zh == zl
    same_feat = [
        me.at(zh=(zh + i) % 2, x=(x + j) % 4, c=(c + k) % 2)
        for i in (1, 0) for j in (2, 1, 3, 0) for k in (0, 1)
    ][:-2] + [me.at(c=1 - c)]
    same_dp = [me.at(zl=(zl + i) % 2, y=(y + j) % 4) for i in (1, 0) for j in (2, 1, 3, 0)][:-1]
    partners = same_feat + same_dp
    partners += [me.at(c=1 - c, y=(y + i) % 4) for i in range(1, 4)]
    partners += [me.at(zh=zl, x=(x + i) % 4, zl=zh) for i in range(1, 4)]
    mirror = me.at(zh=zl, zl=zh)
    for t in partners:
        signal(t)

    @pl.when(jnp.logical_not(still))
    def _():
        signal(mirror)

    pl.semaphore_wait(pltpu.get_barrier_semaphore(), len(partners) + jnp.where(still, 0, 1))

    phase1, owns = [[], []], []
    for half in range(2):
        for dj in (2, 1, 3, 0):
            for dv in (0, 1):
                v, j = (c + dv) % 2, (y + dj) % 4
                src = x_ref.at[v, pl.ds(pl.multiple_of(j * 32 + half * 16, 16), 16)]
                dst = st.at[y, pl.ds(pl.multiple_of(half * 32 + c * 16, 16), 16)]
                if dj == 0 and dv == 0:
                    copy = pltpu.make_async_copy(src, dst, p1_r.at[half, 0, 0])
                    owns.append(copy)
                else:
                    copy = remote(
                        src, dst, p1_s.at[half, dj, dv], p1_r.at[half, dj, dv], me.at(c=v, y=j)
                    )
                    phase1[half].append(copy)
                copy.start()
    own_rows = aligned(c, 512)
    wf[own_rows, :] = w_ref[...].astype(BF)
    wcopy = remote(wf.at[own_rows], wf.at[own_rows], v_s, v_r, me.at(c=1 - c))
    wcopy.start()
    phase2 = [[], []]
    for half in range(2):
        for copy in phase1[half]:
            copy.wait_recv()
        owns[half].wait()
        landing = pl.ds(pl.multiple_of((zh * 4 + y) * 256 + half * 128 + x * 32, 32), 32)
        part = pl.ds(half * 32, 32)
        for dx in (2, 1, 3, 0):
            xt = (x + dx) % 4
            copy = remote(
                st.at[xt, part], xg.at[landing], p2_s.at[half, dx], p2_r.at[half, x], me.at(zh=zl, x=xt, zl=zh)
            )
            phase2[half].append(copy)
            if dx == 0:
                @pl.when(still)
                def _():
                    pltpu.make_async_copy(st.at[x, part], xg.at[landing], p2_r.at[half, x]).start()

                @pl.when(jnp.logical_not(still))
                def _():
                    copy.start()
            else:
                copy.start()

    ag = Gather(
        zl, y, lambda q, r: me.at(zl=q, y=r),
        lambda b, k: xg.at[pl.ds(pl.multiple_of(b * 256 + k * 64, 64), 64)], ag_s, ag_r,
    )
    order = [f] + ag.blocks
    up, down, far = (x + 1) % 4, (x + 3) % 4, (x + 2) % 4
    units, via_copies, ring_copies, zcopies = [], [], [], []

    def span(o, h, size=128, at=0):
        return pl.ds(pl.multiple_of(order[o] * 256 + (h * 128 + at), 64), size)

    def product(o, h):
        u = len(units)
        rows = span(o, h)

        @pl.loop(0, 4)
        def _(j):
            part = jnp.dot(xg[rows, :], wf[:, aligned(j, 256)], preferred_element_type=F32).astype(BF)
            ys[2 * (j % 2), j // 2, rows, :] = part[:, :128]
            ys[2 * (j % 2) + 1, j // 2, rows, :] = part[:, 128:]

        pair = []
        for way, to in ((0, up), (1, down)):
            copy = remote(
                ys.at[far, :, span(o, h, 64, 64 * way)], via.at[way, :, pl.ds(u * 64, 64)],
                via_s.at[way, u], via_r.at[way, u], me.at(x=to),
            )
            copy.start()
            pair.append(copy)
        units.append((o, h))
        via_copies.append(pair)

    def pass_on(u):
        o, h = units[u]
        rows = span(o, h)
        pair = []
        for way, to in ((0, up), (1, down)):
            via_copies[u][way].wait_recv()
            part = span(o, h, 64, 64 * way)
            for side in range(2):
                ys[to, side, part, :] = (
                    ys[to, side, part, :].astype(F32) + via[way, side, pl.ds(u * 64, 64), :].astype(F32)
                ).astype(BF)
            copy = remote(
                ys.at[to, :, rows], yr.at[way, :, rows], rs_s.at[way, u], rs_r.at[way, u], me.at(x=to)
            )
            copy.start()
            pair.append(copy)
        ring_copies.append(pair)

    def settle(u):
        rows = span(*units[u])
        for copy in ring_copies[u]:
            copy.wait_recv()

        def total(side):
            s = ys[x, side, rows, :].astype(F32)
            return s + yr[0, side, rows, :].astype(F32) + yr[1, side, rows, :].astype(F32)

        zs[rows, :] = total(1 - zh).astype(BF)
        copy = remote(zs.at[rows], zr.at[rows], z_s.at[u], z_r.at[u], me.at(zh=1 - zh))
        copy.start()
        zcopies.append(copy)
        yacc[rows, :] = total(zh)

    def push(o, h):
        product(o, h)
        u = len(units) - 1
        if u >= 1:
            pass_on(u - 1)
        if u >= 4:
            settle(u - 4)

    for k in range(NCH):
        for i in range(2):
            ref = xg.at[pl.ds(pl.multiple_of(f * 256 + k * 64 + i * 32, 32), 32)]
            pltpu.make_async_copy(ref, ref, p2_r.at[k // 2, 2 * (k % 2) + i]).wait()
        ag.own(k)
        if k == 1:
            wcopy.wait_recv()
            push(0, 0)
    push(0, 1)
    for h in range(2):
        for k in (2 * h, 2 * h + 1):
            ag.near(k)
            ag.turn(k)
        for o in (1, 2, 3):
            push(o, h)
    for step in ((0, 1), (2, 3)):
        h = step[0] // 2
        for k in step:
            ag.far(k)
        push(4, h)
        if h == 1:
            ag.last(0)
            ag.last(1)
            push(7, 0)
        for k in step:
            ag.rest(k)
        push(5, h)
        push(6, h)
    ag.last(2)
    ag.last(3)
    push(7, 1)
    pass_on(15)
    for u in range(12, 16):
        settle(u)
    for copy in zcopies:
        copy.wait_recv()
    outputs = yacc[...] + zr[...].astype(F32)
    average = jnp.sum(outputs, 0, keepdims=True) / n
    centered = outputs - average
    variance = jnp.sum(centered * centered, 0, keepdims=True) / n
    inverse = lax.rsqrt(variance + EPSILON)

    mine, crossing = jnp.where(c == 0, p, f), jnp.where(c == 0, f, p)
    hh = Gather(
        mine // 4, mine % 4, lambda q, r: me.along(q * 4 + r),
        lambda b, k: hg.at[pl.ds(k * 512, 512), aligned(b, 128)], h_s, h_r, NCH, (1,),
    )
    for k in range(NCH):
        rows = slice(k * 512, (k + 1) * 512)
        normed = centered[rows] * inverse
        hg[rows, aligned(mine, 128)] = normed.astype(BF)
        hh.own(k)
        normed_ref[rows, :] = normed
        half_ref[rows, :] = normed.astype(BF)
    swap = remote(half_ref, hother, c_s, c_r, me.at(c=1 - c))
    swap.start()
    squares = jnp.sum(w_ref[...] * w_ref[...], 0, keepdims=True)
    for step in (hh.near, hh.turn, hh.far, hh.rest, hh.last):
        for k in range(NCH):
            step(k)

    gcopies = [[], []]
    for step in range(2):
        side = (1 - crossing // 4) if step == 0 else crossing // 4
        gs[side] = lax.dot_general(
            hg[aligned(side, 1024), :], hg[aligned(mine, 256), :],
            (((1,), (1,)), ((), ())), preferred_element_type=F32,
        ).astype(BF).reshape(4, 256, 256)
        for i in (2, 1, 3, 0):
            t = (crossing + i) % 4
            copy = remote(
                gs.at[side, t], gr.at[i, side], g_s.at[step, i], g_r.at[step, i],
                me.across_swapped((crossing // 4) * 4 + t),
            )
            copy.start()
            gcopies[step].append(copy)
    swap.wait_recv()
    corr = jnp.sum(half_ref[...].astype(F32) * hother[...].astype(F32), 0, keepdims=True) / n
    extra = (-2.0 * (1.0 - corr) - 2.0 * REDUNDANCY * corr) / n
    q = mine // 4
    other = 1 - q

    def gram_total(side):
        for copy in gcopies[0 if side is other else 1]:
            copy.wait_recv()
        s = gr[0, side].astype(F32)
        for i in range(1, 4):
            s = s + gr[i, side].astype(F32)
        return s

    gzs[...] = gram_total(other).astype(BF)
    gzcopy = remote(gzs, gzr, gz_s, gz_r, me.along(other * 4 + mine % 4))
    gzcopy.start()
    keep = gram_total(q)
    gzcopy.wait_recv()
    gram[:, aligned(crossing, 256)] = (keep + gzr[...].astype(F32)).astype(BF)
    gg = Gather(
        crossing // 4, crossing % 4, lambda q, r: me.across(q * 4 + r),
        lambda b, k: gram.at[pl.ds(k * 128, 128), aligned(b, 256)], gg_s, gg_r, 2, (),
    )
    gg.run()

    kappa = 2.0 * REDUNDANCY / (n * n)
    tcopies = []
    member = mine % 2
    for i in (2, 1, 3, 0):
        tile = (mine // 2 + i) % 4
        part = kappa * jnp.dot(gram[...], hg[:, aligned(tile, 256)], preferred_element_type=F32)
        ts[2 * tile] = part[:, :128].astype(BF)
        ts[2 * tile + 1] = part[:, 128:].astype(BF)
        for side in range(2):
            to = 2 * tile + side
            if i == 0:
                to = mine + 1 - 2 * member
            if i != 0 or side == 0:
                copy = remote(
                    ts.at[to], tr.at[aligned(mine, 256)], t_s.at[i, side], t_r.at[i, member], me.along(to)
                )
                copy.start()
                tcopies.append(copy)
    tr[aligned(mine, 256), :] = ts[mine]
    ref = ts.at[0]
    for i in (0, 1, 2, 3):
        if i == 0:
            pltpu.make_async_copy(ref, ref, t_r.at[0, 1 - member]).wait()
        else:
            for side in range(2):
                pltpu.make_async_copy(ref, ref, t_r.at[i, side]).wait()
    grads = tr[...].astype(F32) + extra * hother[...].astype(F32)
    normed = normed_ref[...]
    mean = jnp.sum(grads, 0, keepdims=True) / n
    cross = jnp.sum(grads * normed, 0, keepdims=True) / n

    oo = Gather(
        zh, x, lambda q, r: me.at(zh=q, x=r),
        lambda b, k: og.at[pl.ds(k * 512, 512), aligned(b, 128)], o_s, o_r,
    )
    for k in range(NCH):
        rows = slice(k * 512, (k + 1) * 512)
        og[rows, aligned(p, 128)] = (inverse * (grads[rows] - mean - normed[rows] * cross)).astype(BF)
        oo.own(k)
    for step in (oo.near, oo.turn, oo.far):
        for k in range(NCH):
            step(k)
    near_cols, far_cols = aligned(zh, 512), aligned(1 - zh, 512)

    @pl.loop(0, 4)
    def _(m):
        cols = aligned(m, 256)
        wacc[cols, near_cols] = lax.dot_general(
            xg[:, cols], og[:, near_cols], (((0,), (0,)), ((), ())), preferred_element_type=F32
        )

    gcopies2 = []
    for k in range(NCH):
        oo.rest(k)
        oo.last(k)
        rows = pl.ds(k * 512, 512)
        for side in range(2):
            core = (1 - c) if side == 0 else c
            for m in range(2):
                cols = aligned(core * 2 + m, 256)
                part = lax.dot_general(
                    xg[rows, cols], og[rows, far_cols], (((0,), (0,)), ((), ())), preferred_element_type=F32
                )
                if k == 0:
                    wacc[cols, far_cols] = part
                else:
                    wacc[cols, far_cols] += part
                if k == NCH - 1 and side == 0:
                    copy = remote(
                        wacc.at[cols], wrecv.at[pl.ds(m * 256, 256)], w_s.at[m], w_r.at[m], me.at(c=1 - c)
                    )
                    copy.start()
                    gcopies2.append(copy)
    for copy in gcopies2:
        copy.wait_recv()
    wg = wacc[aligned(c, 512), :] + wrecv[...]
    wg_ref[...] = wg
    grad_squares = jnp.sum(wg * wg, 0, keepdims=True)

    def fold(v):
        s = v[:, :128]
        for i in range(1, 8):
            s = s + v[:, i * 128:(i + 1) * 128]
        return s

    msg[...] = jnp.zeros_like(msg)
    msg[0:1, :] = fold(grad_squares)
    msg[1:2, :] = fold(squares)
    ncopies = []
    for i, to in enumerate(same_feat):
        copy = remote(msg, got.at[i], n_s.at[i], n_r.at[i], to)
        copy.start()
        ncopies.append(copy)
    s = msg[...]
    for i, copy in enumerate(ncopies):
        copy.wait_recv()
        s = s + got[i]
    mid[...] = s
    mcopies = []
    for i, to in enumerate(same_dp):
        copy = remote(mid, got2.at[i], m_s.at[i], m_r.at[i], to)
        copy.start()
        mcopies.append(copy)
    for i, copy in enumerate(mcopies):
        copy.wait_recv()
        s = s + got2[i]
    sums = jnp.sqrt(jnp.sum(s, 1, keepdims=True))
    trust_ref[...] = jnp.broadcast_to(sums[1:2, :] / (sums[0:1, :] + NORM_EPSILON), (8, 128))
    for copy in [swap, gzcopy, wcopy] + gcopies2 + sum(via_copies + ring_copies, []) + zcopies + gcopies[0] + gcopies[1] + tcopies + ncopies + mcopies:
        copy.wait_send()
    for copy in phase1[0] + phase1[1] + phase2[0][:3] + phase2[1][:3]:
        copy.wait_send()

    @pl.when(jnp.logical_not(still))
    def _():
        phase2[0][3].wait_send()
        phase2[1][3].wait_send()

    for g in (ag, hh, gg, oo):
        g.close()


def vmem(n):
    return [pl.BlockSpec(memory_space=pltpu.VMEM)] * n


def gradient(view_features, weight):
    dma = pltpu.SemaphoreType.DMA

    def v(*shape, kind=BF):
        return pltpu.VMEM(shape, kind)

    def two(*shape):
        return [dma(shape) if shape else dma] * 2

    return pl.pallas_call(
        kernel,
        out_shape=(
            jax.ShapeDtypeStruct((512, 1024), F32),
            jax.ShapeDtypeStruct((8, 128), F32),
        ),
        in_specs=vmem(2),
        out_specs=tuple(vmem(2)),
        scratch_shapes=[
            v(4, 64, 1024), v(2048, 1024), v(1024, 1024), v(4, 2, 2048, 128), v(2, 2, 1024, 128), v(2, 2, 2048, 128),
            v(2048, 128), v(2048, 128), v(2048, 128, kind=F32), v(2048, 128, kind=F32), v(2048, 128),
            v(2048, 1024), v(2048, 128), v(2, 4, 256, 256), v(4, 2, 256, 256), v(256, 256), v(256, 256),
            v(256, 2048), v(8, 256, 128), v(2048, 128), v(2048, 1024), v(1024, 1024, kind=F32),
            v(512, 1024, kind=F32), v(8, 128, kind=F32), v(15, 8, 128, kind=F32), v(8, 128, kind=F32),
            v(7, 8, 128, kind=F32),
            *two(2, 4, 2), *two(2, 4), *two(), *two(7, NCH), *two(2, 16), *two(2, 16), *two(16),
            *two(), *two(7, NCH), *two(2, 4), *two(), *two(7, 2), *two(4, 2), *two(7, NCH), *two(2), *two(15), *two(7),
        ],
        compiler_params=pltpu.CompilerParams(
            collective_id=0, has_side_effects=True, vmem_limit_bytes=60 * 2**20
        ),
    )(view_features, weight)


def update_kernel(trust_ref, wg_ref, w_ref, v_ref, nw_ref, nv_ref):
    new_velocity = MOMENTUM * v_ref[...] + trust_ref[0:1, 0:1] * wg_ref[...]
    nv_ref[...] = new_velocity
    nw_ref[...] = w_ref[...] - LEARN_RATE * new_velocity


def update(trust, wg, weight, velocity):
    block = pl.BlockSpec((256, 1024), lambda i: (i, 0))
    return pl.pallas_call(
        update_kernel,
        grid=(2,),
        out_shape=(jax.ShapeDtypeStruct((512, 1024), F32),) * 2,
        in_specs=[pl.BlockSpec((8, 128), lambda i: (0, 0)), block, block, block],
        out_specs=(block, block),
    )(trust, wg, weight, velocity)


def per_device(view_features, weight, velocity):
    wg, trust = gradient(view_features, weight)
    return update(trust, wg, weight, velocity)


def solution(mesh):
    in_specs = (P(None, "dp", "feat"), P("dp", "feat"), P("dp", "feat"))
    out_specs = (P("dp", "feat"), P("dp", "feat"))
    return jax.shard_map(
        per_device, mesh=mesh, in_specs=in_specs, out_specs=out_specs, check_vma=False
    )
```

```python
import functools

import jax
import jax.numpy as jnp
from jax import lax
from jax.experimental import pallas as pl
from jax.experimental.pallas import tpu as pltpu
from jax.sharding import PartitionSpec as P

EPSILON = 1e-05
NORM_EPSILON = 1e-06
REDUNDANCY = 0.0051
MOMENTUM = 0.9
LEARN_RATE = 0.2
MESH = pl.DeviceIdType.MESH
BF = jnp.bfloat16
F32 = jnp.float32
NCH = 4


class Place:
    def __init__(self):
        d, f = lax.axis_index("dp"), lax.axis_index("feat")
        self.d, self.f, self.p = d, f, d // 2
        self.zh, self.x, self.c = d // 8, (d // 2) % 4, d % 2
        self.zl, self.y = f // 4, f % 4

    def at(self, zh=None, x=None, c=None, zl=None, y=None):
        zh = self.zh if zh is None else zh
        x = self.x if x is None else x
        c = self.c if c is None else c
        zl = self.zl if zl is None else zl
        y = self.y if y is None else y
        return ((zh * 4 + x) * 2 + c, zl * 4 + y)

    def along(self, i):
        zero = self.c == 0
        return (jnp.where(zero, i * 2, self.d), jnp.where(zero, self.f, i))

    def across(self, i):
        zero = self.c == 0
        return (jnp.where(zero, self.d, i * 2 + 1), jnp.where(zero, i, self.f))

    def across_swapped(self, i):
        zero = self.c == 0
        return (jnp.where(zero, self.d + 1, i * 2), jnp.where(zero, i, self.f))


def signal(target):
    pl.semaphore_signal(
        pltpu.get_barrier_semaphore(), inc=1, device_id=target, device_id_type=MESH
    )


def remote(src, dst, send, recv, target):
    return pltpu.make_async_remote_copy(
        src_ref=src, dst_ref=dst, send_sem=send, recv_sem=recv, device_id=target, device_id_type=MESH
    )


class Gather:
    def __init__(self, q, r, device, piece, send, recv, count=NCH, paired=range(NCH)):
        up, down, far, other = (r + 1) % 4, (r + 3) % 4, (r + 2) % 4, 1 - q
        self.blocks = [
            other * 4 + r, q * 4 + down, q * 4 + up, q * 4 + far,
            other * 4 + down, other * 4 + up, other * 4 + far,
        ]
        mine = q * 4 + r
        self.paired = paired
        self.count = count

        def make(block, k, slot, target):
            ref = piece(block, k)
            return remote(ref, ref, send.at[slot, k], recv.at[slot, k], target)

        to_up, to_down, to_pair = device(q, up), device(q, down), device(other, r)
        self.copies = []
        for k in range(count):
            if k in paired:
                last = make(self.blocks[3], k, 6, to_pair)
            elif k % 2 == 0:
                last = make(self.blocks[4], k, 6, to_up)
            else:
                last = make(self.blocks[5], k, 6, to_down)
            self.copies.append([
                make(mine, k, 0, to_pair),
                make(mine, k, 1, to_up),
                make(mine, k, 2, to_down),
                make(self.blocks[1], k, 3, to_up) if k % 2 == 0 else make(self.blocks[2], k, 3, to_down),
                make(self.blocks[0], k, 4, to_up),
                make(self.blocks[0], k, 5, to_down),
                last,
            ])

    def own(self, k):
        for slot in (0, 1, 2):
            self.copies[k][slot].start()

    def near(self, k):
        c = self.copies[k]
        first = 1 + k % 2
        c[first].wait_recv()
        c[3].start()
        c[3 - first].wait_recv()

    def turn(self, k):
        c = self.copies[k]
        c[0].wait_recv()
        c[4].start()
        c[5].start()

    def far(self, k):
        c = self.copies[k]
        if k in self.paired:
            c[3].wait_recv()
            c[6].start()

    def rest(self, k):
        c = self.copies[k]
        if k not in self.paired:
            c[4 + k % 2].wait_recv()
            c[6].start()
            c[3].wait_recv()
            c[5 - k % 2].wait_recv()
        else:
            c[4].wait_recv()
            c[5].wait_recv()

    def last(self, k):
        self.copies[k][6].wait_recv()

    def run(self):
        for step in (self.own, self.near, self.turn, self.far, self.rest, self.last):
            for k in range(self.count):
                step(k)

    def close(self):
        for c in self.copies:
            for copy in c:
                copy.wait_send()


def aligned(i, size):
    return pl.ds(pl.multiple_of(i * size, size), size)


def kernel(
    x_ref, w_ref, wg_ref, trust_ref,
    st, xg, wf, ys, via, yr, zs, zr, yacc, normed_ref, half_ref,
    hg, hother, gs, gr, gzs, gzr, gram, ts, tr, og, wacc, wrecv, msg, got, mid, got2,
    p1_s, p1_r, p2_s, p2_r, v_s, v_r, ag_s, ag_r, via_s, via_r, rs_s, rs_r, z_s, z_r,
    c_s, c_r, h_s, h_r, g_s, g_r, gz_s, gz_r, gg_s, gg_r, t_s, t_r, o_s, o_r, w_s, w_r, n_s, n_r, m_s, m_r,
):
    me = Place()
    d, p, f, c, x, y, zh, zl = me.d, me.p, me.f, me.c, me.x, me.y, me.zh, me.zl
    n = 2048
    still = zh == zl
    same_feat = [
        me.at(zh=(zh + i) % 2, x=(x + j) % 4, c=(c + k) % 2)
        for i in (1, 0) for j in (2, 1, 3, 0) for k in (0, 1)
    ][:-2] + [me.at(c=1 - c)]
    same_dp = [me.at(zl=(zl + i) % 2, y=(y + j) % 4) for i in (1, 0) for j in (2, 1, 3, 0)][:-1]
    partners = same_feat + same_dp
    partners += [me.at(c=1 - c, y=(y + i) % 4) for i in range(1, 4)]
    partners += [me.at(zh=zl, x=(x + i) % 4, zl=zh) for i in range(1, 4)]
    mirror = me.at(zh=zl, zl=zh)
    for t in partners:
        signal(t)

    @pl.when(jnp.logical_not(still))
    def _():
        signal(mirror)

    pl.semaphore_wait(pltpu.get_barrier_semaphore(), len(partners) + jnp.where(still, 0, 1))

    phase1, owns = [[], []], []
    for half in range(2):
        for dj in (2, 1, 3, 0):
            for dv in (0, 1):
                v, j = (c + dv) % 2, (y + dj) % 4
                src = x_ref.at[v, pl.ds(pl.multiple_of(j * 32 + half * 16, 16), 16)]
                dst = st.at[y, pl.ds(pl.multiple_of(half * 32 + c * 16, 16), 16)]
                if dj == 0 and dv == 0:
                    copy = pltpu.make_async_copy(src, dst, p1_r.at[half, 0, 0])
                    owns.append(copy)
                else:
                    copy = remote(
                        src, dst, p1_s.at[half, dj, dv], p1_r.at[half, dj, dv], me.at(c=v, y=j)
                    )
                    phase1[half].append(copy)
                copy.start()
    own_rows = aligned(c, 512)
    wf[own_rows, :] = w_ref[...].astype(BF)
    wcopy = remote(wf.at[own_rows], wf.at[own_rows], v_s, v_r, me.at(c=1 - c))
    wcopy.start()
    phase2 = [[], []]
    for half in range(2):
        for copy in phase1[half]:
            copy.wait_recv()
        owns[half].wait()
        landing = pl.ds(pl.multiple_of((zh * 4 + y) * 256 + half * 128 + x * 32, 32), 32)
        part = pl.ds(half * 32, 32)
        for dx in (2, 1, 3, 0):
            xt = (x + dx) % 4
            copy = remote(
                st.at[xt, part], xg.at[landing], p2_s.at[half, dx], p2_r.at[half, x], me.at(zh=zl, x=xt, zl=zh)
            )
            phase2[half].append(copy)
            if dx == 0:
                @pl.when(still)
                def _():
                    pltpu.make_async_copy(st.at[x, part], xg.at[landing], p2_r.at[half, x]).start()

                @pl.when(jnp.logical_not(still))
                def _():
                    copy.start()
            else:
                copy.start()

    ag = Gather(
        zl, y, lambda q, r: me.at(zl=q, y=r),
        lambda b, k: xg.at[pl.ds(pl.multiple_of(b * 256 + k * 64, 64), 64)], ag_s, ag_r,
    )
    order = [f] + ag.blocks
    up, down, far = (x + 1) % 4, (x + 3) % 4, (x + 2) % 4
    units, via_copies, ring_copies, zcopies = [], [], [], []

    def span(o, h, size=128, at=0):
        return pl.ds(pl.multiple_of(order[o] * 256 + (h * 128 + at), 64), size)

    def product(o, h):
        u = len(units)
        rows = span(o, h)

        @pl.loop(0, 4)
        def _(j):
            part = jnp.dot(xg[rows, :], wf[:, aligned(j, 256)], preferred_element_type=F32).astype(BF)
            ys[2 * (j % 2), j // 2, rows, :] = part[:, :128]
            ys[2 * (j % 2) + 1, j // 2, rows, :] = part[:, 128:]

        pair = []
        for way, to in ((0, up), (1, down)):
            copy = remote(
                ys.at[far, :, span(o, h, 64, 64 * way)], via.at[way, :, pl.ds(u * 64, 64)],
                via_s.at[way, u], via_r.at[way, u], me.at(x=to),
            )
            copy.start()
            pair.append(copy)
        units.append((o, h))
        via_copies.append(pair)

    def pass_on(u):
        o, h = units[u]
        rows = span(o, h)
        pair = []
        for way, to in ((0, up), (1, down)):
            via_copies[u][way].wait_recv()
            part = span(o, h, 64, 64 * way)
            for side in range(2):
                ys[to, side, part, :] = (
                    ys[to, side, part, :].astype(F32) + via[way, side, pl.ds(u * 64, 64), :].astype(F32)
                ).astype(BF)
            copy = remote(
                ys.at[to, :, rows], yr.at[way, :, rows], rs_s.at[way, u], rs_r.at[way, u], me.at(x=to)
            )
            copy.start()
            pair.append(copy)
        ring_copies.append(pair)

    def settle(u):
        rows = span(*units[u])
        for copy in ring_copies[u]:
            copy.wait_recv()

        def total(side):
            s = ys[x, side, rows, :].astype(F32)
            return s + yr[0, side, rows, :].astype(F32) + yr[1, side, rows, :].astype(F32)

        zs[rows, :] = total(1 - zh).astype(BF)
        copy = remote(zs.at[rows], zr.at[rows], z_s.at[u], z_r.at[u], me.at(zh=1 - zh))
        copy.start()
        zcopies.append(copy)
        yacc[rows, :] = total(zh)

    def push(o, h):
        product(o, h)
        u = len(units) - 1
        if u >= 1:
            pass_on(u - 1)
        if u >= 4:
            settle(u - 4)

    for k in range(NCH):
        for i in range(2):
            ref = xg.at[pl.ds(pl.multiple_of(f * 256 + k * 64 + i * 32, 32), 32)]
            pltpu.make_async_copy(ref, ref, p2_r.at[k // 2, 2 * (k % 2) + i]).wait()
        ag.own(k)
        if k == 1:
            wcopy.wait_recv()
            push(0, 0)
    push(0, 1)
    for h in range(2):
        for k in (2 * h, 2 * h + 1):
            ag.near(k)
            ag.turn(k)
        for o in (1, 2, 3):
            push(o, h)
    for step in ((0, 1), (2, 3)):
        h = step[0] // 2
        for k in step:
            ag.far(k)
        push(4, h)
        if h == 1:
            ag.last(0)
            ag.last(1)
            push(7, 0)
        for k in step:
            ag.rest(k)
        push(5, h)
        push(6, h)
    ag.last(2)
    ag.last(3)
    push(7, 1)
    pass_on(15)
    for u in range(12, 16):
        settle(u)
    for copy in zcopies:
        copy.wait_recv()
    outputs = yacc[...] + zr[...].astype(F32)
    average = jnp.sum(outputs, 0, keepdims=True) / n
    centered = outputs - average
    variance = jnp.sum(centered * centered, 0, keepdims=True) / n
    inverse = lax.rsqrt(variance + EPSILON)

    mine, crossing = jnp.where(c == 0, p, f), jnp.where(c == 0, f, p)
    hh = Gather(
        mine // 4, mine % 4, lambda q, r: me.along(q * 4 + r),
        lambda b, k: hg.at[pl.ds(k * 512, 512), aligned(b, 128)], h_s, h_r, NCH, (1,),
    )
    for k in range(NCH):
        rows = slice(k * 512, (k + 1) * 512)
        normed = centered[rows] * inverse
        hg[rows, aligned(mine, 128)] = normed.astype(BF)
        hh.own(k)
        normed_ref[rows, :] = normed
        half_ref[rows, :] = normed.astype(BF)
    swap = remote(half_ref, hother, c_s, c_r, me.at(c=1 - c))
    swap.start()
    squares = jnp.sum(w_ref[...] * w_ref[...], 0, keepdims=True)
    for step in (hh.near, hh.turn, hh.far, hh.rest, hh.last):
        for k in range(NCH):
            step(k)

    gcopies = [[], []]
    for step in range(2):
        side = (1 - crossing // 4) if step == 0 else crossing // 4
        gs[side] = lax.dot_general(
            hg[aligned(side, 1024), :], hg[aligned(mine, 256), :],
            (((1,), (1,)), ((), ())), preferred_element_type=F32,
        ).astype(BF).reshape(4, 256, 256)
        for i in (2, 1, 3, 0):
            t = (crossing + i) % 4
            copy = remote(
                gs.at[side, t], gr.at[i, side], g_s.at[step, i], g_r.at[step, i],
                me.across_swapped((crossing // 4) * 4 + t),
            )
            copy.start()
            gcopies[step].append(copy)
    swap.wait_recv()
    corr = jnp.sum(half_ref[...].astype(F32) * hother[...].astype(F32), 0, keepdims=True) / n
    extra = (-2.0 * (1.0 - corr) - 2.0 * REDUNDANCY * corr) / n
    q = mine // 4
    other = 1 - q

    def gram_total(side):
        for copy in gcopies[0 if side is other else 1]:
            copy.wait_recv()
        s = gr[0, side].astype(F32)
        for i in range(1, 4):
            s = s + gr[i, side].astype(F32)
        return s

    gzs[...] = gram_total(other).astype(BF)
    gzcopy = remote(gzs, gzr, gz_s, gz_r, me.along(other * 4 + mine % 4))
    gzcopy.start()
    keep = gram_total(q)
    gzcopy.wait_recv()
    gram[:, aligned(crossing, 256)] = (keep + gzr[...].astype(F32)).astype(BF)
    qc, rc = crossing // 4, crossing % 4
    pair_block = (1 - qc) * 4 + rc
    gg = []
    for k in range(2):
        chunk = []
        for slot in range(7):
            to = pair_block if slot == 0 else qc * 4 + (rc + (2, 1, 3)[(slot - 1) % 3]) % 4
            ref = gram.at[pl.ds(k * 128, 128), aligned(crossing if slot < 4 else pair_block, 256)]
            chunk.append(remote(ref, ref, gg_s.at[slot, k], gg_r.at[slot, k], me.across(to)))
        gg.append(chunk)
        for slot in range(4):
            chunk[slot].start()
    for chunk in gg:
        chunk[0].wait_recv()
        for slot in (4, 5, 6):
            chunk[slot].start()
    for chunk in gg:
        for slot in range(1, 7):
            chunk[slot].wait_recv()

    kappa = 2.0 * REDUNDANCY / (n * n)
    tcopies = []
    member = mine % 2
    for i in (2, 1, 3, 0):
        tile = (mine // 2 + i) % 4
        part = kappa * jnp.dot(gram[...], hg[:, aligned(tile, 256)], preferred_element_type=F32)
        ts[2 * tile] = part[:, :128].astype(BF)
        ts[2 * tile + 1] = part[:, 128:].astype(BF)
        for side in range(2):
            to = 2 * tile + side
            if i == 0:
                to = mine + 1 - 2 * member
            if i != 0 or side == 0:
                copy = remote(
                    ts.at[to], tr.at[aligned(mine, 256)], t_s.at[i, side], t_r.at[i, member], me.along(to)
                )
                copy.start()
                tcopies.append(copy)
    tr[aligned(mine, 256), :] = ts[mine]
    ref = ts.at[0]
    for i in (0, 1, 2, 3):
        if i == 0:
            pltpu.make_async_copy(ref, ref, t_r.at[0, 1 - member]).wait()
        else:
            for side in range(2):
                pltpu.make_async_copy(ref, ref, t_r.at[i, side]).wait()
    grads = tr[...].astype(F32) + extra * hother[...].astype(F32)
    normed = normed_ref[...]
    mean = jnp.sum(grads, 0, keepdims=True) / n
    cross = jnp.sum(grads * normed, 0, keepdims=True) / n

    oo = Gather(
        zh, x, lambda q, r: me.at(zh=q, x=r),
        lambda b, k: og.at[pl.ds(k * 512, 512), aligned(b, 128)], o_s, o_r,
    )
    for k in range(NCH):
        rows = slice(k * 512, (k + 1) * 512)
        og[rows, aligned(p, 128)] = (inverse * (grads[rows] - mean - normed[rows] * cross)).astype(BF)
        oo.own(k)
    for step in (oo.near, oo.turn, oo.far):
        for k in range(NCH):
            step(k)
    near_cols, far_cols = aligned(zh, 512), aligned(1 - zh, 512)

    @pl.loop(0, 4)
    def _(m):
        cols = aligned(m, 256)
        wacc[cols, near_cols] = lax.dot_general(
            xg[:, cols], og[:, near_cols], (((0,), (0,)), ((), ())), preferred_element_type=F32
        )

    gcopies2 = []
    for k in range(NCH):
        oo.rest(k)
        oo.last(k)
        rows = pl.ds(k * 512, 512)
        for side in range(2):
            core = (1 - c) if side == 0 else c
            for m in range(2):
                cols = aligned(core * 2 + m, 256)
                part = lax.dot_general(
                    xg[rows, cols], og[rows, far_cols], (((0,), (0,)), ((), ())), preferred_element_type=F32
                )
                if k == 0:
                    wacc[cols, far_cols] = part
                else:
                    wacc[cols, far_cols] += part
                if k == NCH - 1 and side == 0:
                    copy = remote(
                        wacc.at[cols], wrecv.at[pl.ds(m * 256, 256)], w_s.at[m], w_r.at[m], me.at(c=1 - c)
                    )
                    copy.start()
                    gcopies2.append(copy)
    for copy in gcopies2:
        copy.wait_recv()
    wg = wacc[aligned(c, 512), :] + wrecv[...]
    wg_ref[...] = wg
    grad_squares = jnp.sum(wg * wg, 0, keepdims=True)

    def fold(v):
        s = v[:, :128]
        for i in range(1, 8):
            s = s + v[:, i * 128:(i + 1) * 128]
        return s

    msg[...] = jnp.zeros_like(msg)
    msg[0:1, :] = fold(grad_squares)
    msg[1:2, :] = fold(squares)
    ncopies = []
    for i, to in enumerate(same_feat):
        copy = remote(msg, got.at[i], n_s.at[i], n_r.at[i], to)
        copy.start()
        ncopies.append(copy)
    s = msg[...]
    for i, copy in enumerate(ncopies):
        copy.wait_recv()
        s = s + got[i]
    mid[...] = s
    mcopies = []
    for i, to in enumerate(same_dp):
        copy = remote(mid, got2.at[i], m_s.at[i], m_r.at[i], to)
        copy.start()
        mcopies.append(copy)
    for i, copy in enumerate(mcopies):
        copy.wait_recv()
        s = s + got2[i]
    sums = jnp.sqrt(jnp.sum(s, 1, keepdims=True))
    trust_ref[...] = jnp.broadcast_to(sums[1:2, :] / (sums[0:1, :] + NORM_EPSILON), (8, 128))
    for copy in [swap, gzcopy, wcopy] + gcopies2 + sum(via_copies + ring_copies, []) + zcopies + gcopies[0] + gcopies[1] + sum(gg, []) + tcopies + ncopies + mcopies:
        copy.wait_send()
    for copy in phase1[0] + phase1[1] + phase2[0][:3] + phase2[1][:3]:
        copy.wait_send()

    @pl.when(jnp.logical_not(still))
    def _():
        phase2[0][3].wait_send()
        phase2[1][3].wait_send()

    for g in (ag, hh, oo):
        g.close()


def vmem(n):
    return [pl.BlockSpec(memory_space=pltpu.VMEM)] * n


def gradient(view_features, weight):
    dma = pltpu.SemaphoreType.DMA

    def v(*shape, kind=BF):
        return pltpu.VMEM(shape, kind)

    def two(*shape):
        return [dma(shape) if shape else dma] * 2

    return pl.pallas_call(
        kernel,
        out_shape=(
            jax.ShapeDtypeStruct((512, 1024), F32),
            jax.ShapeDtypeStruct((8, 128), F32),
        ),
        in_specs=vmem(2),
        out_specs=tuple(vmem(2)),
        scratch_shapes=[
            v(4, 64, 1024), v(2048, 1024), v(1024, 1024), v(4, 2, 2048, 128), v(2, 2, 1024, 128), v(2, 2, 2048, 128),
            v(2048, 128), v(2048, 128), v(2048, 128, kind=F32), v(2048, 128, kind=F32), v(2048, 128),
            v(2048, 1024), v(2048, 128), v(2, 4, 256, 256), v(4, 2, 256, 256), v(256, 256), v(256, 256),
            v(256, 2048), v(8, 256, 128), v(2048, 128), v(2048, 1024), v(1024, 1024, kind=F32),
            v(512, 1024, kind=F32), v(8, 128, kind=F32), v(15, 8, 128, kind=F32), v(8, 128, kind=F32),
            v(7, 8, 128, kind=F32),
            *two(2, 4, 2), *two(2, 4), *two(), *two(7, NCH), *two(2, 16), *two(2, 16), *two(16),
            *two(), *two(7, NCH), *two(2, 4), *two(), *two(7, 2), *two(4, 2), *two(7, NCH), *two(2), *two(15), *two(7),
        ],
        compiler_params=pltpu.CompilerParams(
            collective_id=0, has_side_effects=True, vmem_limit_bytes=60 * 2**20
        ),
    )(view_features, weight)


def update_kernel(trust_ref, wg_ref, w_ref, v_ref, nw_ref, nv_ref):
    new_velocity = MOMENTUM * v_ref[...] + trust_ref[0:1, 0:1] * wg_ref[...]
    nv_ref[...] = new_velocity
    nw_ref[...] = w_ref[...] - LEARN_RATE * new_velocity


def update(trust, wg, weight, velocity):
    block = pl.BlockSpec((256, 1024), lambda i: (i, 0))
    return pl.pallas_call(
        update_kernel,
        grid=(2,),
        out_shape=(jax.ShapeDtypeStruct((512, 1024), F32),) * 2,
        in_specs=[pl.BlockSpec((8, 128), lambda i: (0, 0)), block, block, block],
        out_specs=(block, block),
    )(trust, wg, weight, velocity)


def per_device(view_features, weight, velocity):
    wg, trust = gradient(view_features, weight)
    return update(trust, wg, weight, velocity)


def solution(mesh):
    in_specs = (P(None, "dp", "feat"), P("dp", "feat"), P("dp", "feat"))
    out_specs = (P("dp", "feat"), P("dp", "feat"))
    return jax.shard_map(
        per_device, mesh=mesh, in_specs=in_specs, out_specs=out_specs, check_vma=False
    )
```
